512 devices in a mesh: leaf: 64 (over z, y), sec: 8 (over x, core).
Axes of the slice: x: 4, y: 4, z: 16, core: 2. Of those that a mesh axis runs over, the one named last changes fastest.
Arguments:
- leaf_inv: bfloat16 [524288, 1024], P(('leaf', 'sec')), may hold values from -0.1875 to 0.1875
- subtree_blocks: int32 [64, 8], P('leaf', 'sec'), may hold values from 1 to 8
- subtree_shift_rhs: bfloat16 [524288, 128], P(('leaf', 'sec')), may hold values from -6 to 6
- leaf_noise: bfloat16 [524288, 128], P(('leaf', 'sec')), may hold values from -6 to 6
- leaf_dev: bfloat16 [524288], P(('leaf', 'sec')), may hold values from 0.29882812 to 3
- sep_inv: bfloat16 [16384, 3584], P(('leaf', 'sec')), may hold values from -0.1875 to 0.1875
- sep_panel: bfloat16 [16384, 3584], P(('leaf', 'sec')), may hold values from -0.1875 to 0.1875
- sep_rhs: bfloat16 [3, 16384, 128], P(None, ('leaf', 'sec')), may hold values from -6 to 6
- sep_noise: bfloat16 [3, 16384, 128], P(None, ('leaf', 'sec')), may hold values from -6 to 6
- sep_dev: bfloat16 [3, 16384], P(None, ('leaf', 'sec')), may hold values from 0.29882812 to 3
Outputs:
- subtree_scaled_samples: bfloat16 [524288, 128], P(('leaf', 'sec'))
- sep_sample: bfloat16 [3, 16384, 128], P(None, ('leaf', 'sec'))
The draws below stay inside these ranges and needn't reach their ends.
All inputs are finite; a program needn't handle non-finite values.
Results may differ from the reference program's by a relative error of at most 0.019.
Values may be sent and summed in bfloat16 or wider, within the bound.
A program may use at most 64 MiB of HBM per device.

```python
import math
import jax
import jax.numpy as jnp
from jax import lax

SUBTREE_ROWS = 1024
SEP_DEV = 32
SAMPLE_COUNT = 128
LEVELS = 3
BLOCK = 128
LEAF_ROWS = 524288
SEP_ROWS = 16384
PANEL_COLS = 3584
N_LEAF = 64
N_SEC = 8


def place_ends(drawn, stream_key, low, high):
    place = [jax.random.randint(jax.random.fold_in(stream_key, axis), (), 0, length) for axis, length in enumerate(drawn.shape)]
    main_axis = drawn.shape.index(max(drawn.shape))
    beside = place[:main_axis] + [(place[main_axis] + 1) % drawn.shape[main_axis]] + place[main_axis + 1:]
    return drawn.at[tuple(place)].set(low).at[tuple(beside)].set(high)


def steps_of(rng, dims, cuts, low, high):
    factor_of = 1.0
    for position, blocks in cuts:
        draws = jax.random.uniform(jax.random.fold_in(jax.random.fold_in(rng, 6), position), (blocks,), jnp.float32, low / len(cuts), high / len(cuts))
        factor_of = factor_of * jnp.repeat(jnp.exp(draws), dims[position] // blocks).reshape((-1,) + (1,) * (len(dims) - 1 - position))
    return factor_of


def normal_values(rng, dims, deviation, bound, cuts=(), kind=jnp.bfloat16):
    values = jax.random.normal(rng, dims, jnp.float32) * deviation
    if len(cuts) > 0:
        values = steps_of(rng, dims, cuts, -0.22, 0.18) * values
    return jnp.clip(values, min=-bound, max=bound).astype(kind)


def setup_inputs(seed: int = 0) -> dict:
    key_of = jax.random.split(jax.random.key(seed), 11)
    return {
        "leaf_inv": normal_values(key_of[0], (LEAF_ROWS, SUBTREE_ROWS), SUBTREE_ROWS ** -0.5, 0.1875, ((0, 512),)),
        "subtree_blocks": place_ends(jax.random.randint(key_of[1], (N_LEAF, N_SEC), 1, SUBTREE_ROWS // BLOCK + 1), jax.random.fold_in(key_of[1], 1), 1, (SUBTREE_ROWS // BLOCK + 1) - 1).astype(jnp.int32),
        "subtree_shift_rhs": normal_values(key_of[2], (LEAF_ROWS, SAMPLE_COUNT), 1.0, 6.0, ((0, 512),)),
        "leaf_noise": normal_values(key_of[3], (LEAF_ROWS, SAMPLE_COUNT), 1.0, 6.0, ((0, 512),)),
        "leaf_dev": jnp.clip(jnp.exp(math.log(3.0) - 2.306499 * jax.random.uniform(key_of[4], (LEAF_ROWS,), jnp.float32) ** steps_of(key_of[4], (LEAF_ROWS,), ((0, 512),), -0.2, 0.2)), 0.29882812, 3.0).astype(jnp.bfloat16),
        "sep_inv": normal_values(key_of[5], (SEP_ROWS, PANEL_COLS), (4 * N_SEC * SEP_DEV) ** -0.5, 0.1875, ((0, 512),)),
        "sep_panel": normal_values(key_of[6], (SEP_ROWS, PANEL_COLS), (4 * N_SEC * SEP_DEV) ** -0.5, 0.1875, ((0, 512),)),
        "sep_rhs": normal_values(key_of[7], (LEVELS, SEP_ROWS, SAMPLE_COUNT), 1.0, 6.0, ((1, 512),)),
        "sep_noise": normal_values(key_of[8], (LEVELS, SEP_ROWS, SAMPLE_COUNT), 1.0, 6.0, ((1, 512),)),
        "sep_dev": jnp.clip(jnp.exp(math.log(3.0) - 2.306499 * jax.random.uniform(key_of[9], (LEVELS, SEP_ROWS), jnp.float32) ** steps_of(key_of[9], (LEVELS, SEP_ROWS), ((1, 512),), -0.2, 0.2)), 0.29882812, 3.0).astype(jnp.bfloat16),
    }


def subtree_forward(matrix_entries):
    inverse_block, mean_shifted, row_activity = matrix_entries
    block_product = jnp.dot(inverse_block, mean_shifted, preferred_element_type=jnp.float32)
    return jnp.where(row_activity, block_product, jnp.float32(0.0)).astype(jnp.bfloat16)


def sep_forward(matrix_entries):
    panel, inverse_block, mean_shifted, children = matrix_entries
    reduced = (mean_shifted.astype(jnp.float32) - jnp.dot(panel, children, preferred_element_type=jnp.float32)).astype(jnp.bfloat16)
    return jnp.dot(inverse_block, reduced, preferred_element_type=jnp.float32).astype(jnp.bfloat16)


def solve_back(matrix_entries):
    inverse_block, vector = matrix_entries
    return jnp.dot(inverse_block.T, vector, preferred_element_type=jnp.float32).astype(jnp.bfloat16)


def push_down(matrix_entries):
    panel, vector = matrix_entries
    return jnp.dot(panel.T, vector, preferred_element_type=jnp.float32)


def leaf_back(matrix_entries):
    inverse_block, vector = matrix_entries
    return jnp.dot(inverse_block.T, vector, preferred_element_type=jnp.float32)


def reference(leaf_inv, subtree_blocks, subtree_shift_rhs, leaf_noise, leaf_dev, sep_inv, sep_panel, sep_rhs, sep_noise, sep_dev):
    device_list = N_LEAF * N_SEC
    active_rows = subtree_blocks.reshape(device_list).astype(jnp.int32) * BLOCK
    row_positions = jnp.arange(SUBTREE_ROWS, dtype=jnp.int32)
    row_activity = (row_positions[None, :] >= (SUBTREE_ROWS - active_rows)[:, None])[:, :, None]
    inverse_subtree = leaf_inv.reshape(device_list, SUBTREE_ROWS, SUBTREE_ROWS)
    subtree_rhs_block = jnp.where(row_activity, subtree_shift_rhs.reshape(device_list, SUBTREE_ROWS, SAMPLE_COUNT), jnp.zeros((), subtree_shift_rhs.dtype))
    subtree_forward_solution = lax.map(subtree_forward, (inverse_subtree, subtree_rhs_block, row_activity))
    top = subtree_forward_solution[:, SUBTREE_ROWS - SEP_DEV:, :].reshape(device_list * SEP_DEV, SAMPLE_COUNT)
    solved = []
    for height in range(1, LEVELS + 1):
        span = 2 ** height * N_SEC * SEP_DEV
        offset = (2 ** height - 2) * N_SEC * SEP_DEV
        groups = device_list * SEP_DEV // span
        panel = sep_panel[:, offset:offset + span].reshape(groups, span, span)
        inverse_block = sep_inv[:, offset:offset + span].reshape(groups, span, span)
        mean_shifted = sep_rhs[height - 1].reshape(groups, span, SAMPLE_COUNT)
        children = top.reshape(groups, span, SAMPLE_COUNT)
        result = lax.map(sep_forward, (panel, inverse_block, mean_shifted, children)).reshape(device_list * SEP_DEV, SAMPLE_COUNT)
        solved.append(result)
        top = result
    samples = [None] * LEVELS
    correction = jnp.zeros((device_list * SEP_DEV, SAMPLE_COUNT), jnp.float32)
    for height in range(LEVELS, 0, -1):
        span = 2 ** height * N_SEC * SEP_DEV
        offset = (2 ** height - 2) * N_SEC * SEP_DEV
        groups = device_list * SEP_DEV // span
        panel = sep_panel[:, offset:offset + span].reshape(groups, span, span)
        inverse_block = sep_inv[:, offset:offset + span].reshape(groups, span, span)
        summed = solved[height - 1].astype(jnp.float32) + sep_noise[height - 1].astype(jnp.float32) - correction
        vector = summed.astype(jnp.bfloat16).reshape(groups, span, SAMPLE_COUNT)
        backed = lax.map(solve_back, (inverse_block, vector))
        flat = backed.reshape(device_list * SEP_DEV, SAMPLE_COUNT)
        samples[height - 1] = (sep_dev[height - 1][:, None].astype(jnp.float32) * flat.astype(jnp.float32)).astype(jnp.bfloat16)
        correction = lax.map(push_down, (panel, backed)).reshape(device_list * SEP_DEV, SAMPLE_COUNT)
    boundary = correction.reshape(device_list, SEP_DEV, SAMPLE_COUNT)
    leading = jnp.zeros((device_list, SUBTREE_ROWS - SEP_DEV, SAMPLE_COUNT), jnp.float32)
    placed = jnp.concatenate([leading, boundary], axis=1)
    noise_leaf = leaf_noise.reshape(device_list, SUBTREE_ROWS, SAMPLE_COUNT)
    subtree_summed = subtree_forward_solution.astype(jnp.float32) + noise_leaf.astype(jnp.float32) - placed
    subtree_weight = jnp.where(row_activity, subtree_summed, jnp.float32(0.0)).astype(jnp.bfloat16)
    subtree_solution = lax.map(leaf_back, (inverse_subtree, subtree_weight))
    sample_scales = leaf_dev.reshape(device_list, SUBTREE_ROWS, 1).astype(jnp.float32)
    subtree_scaled_samples = jnp.where(row_activity, sample_scales * subtree_solution, jnp.float32(0.0)).astype(jnp.bfloat16).reshape(device_list * SUBTREE_ROWS, SAMPLE_COUNT)
    return subtree_scaled_samples, jnp.stack(samples)
```

```python
import functools

import jax
import jax.numpy as jnp
from jax import lax
from jax.experimental import pallas as pl
from jax.experimental.pallas import tpu as pltpu
from jax.sharding import PartitionSpec as P

MESH = pl.DeviceIdType.MESH
BLOCK = 128
BF = jnp.bfloat16
F32 = jnp.float32
ROWS = 1024
SEP = 32
SECS = 8
SPAN = SECS * SEP
SAMP = 16
NEAR = {1: (1,), 2: (1, 3, 2), 3: (1, 3, 4, 2, 5, 7, 6)}
SEC_PEERS = (6, 4, 7, 5, 2, 3, 1)
X_PEERS = (2, 6, 4)


def dot(a, b, ca, cb):
    return lax.dot_general(a, b, (((ca,), (cb,)), ((), ())), preferred_element_type=F32)


def kernel(
    leaf_inv, blocks, rhs, noise, dev, sep_inv, sep_panel, sep_rhs, sep_noise, sep_dev,
    out, sep_out,
    d_v, rhs_v, noise_v, w_v, x_v, scale_v,
    p1, q1, p2, q2, p3, q3,
    c1_src, c1_buf, rn_src, rn_buf, item_v, f_buf, b_src, b_buf, o_src, o_buf, s_src, s_buf,
    ld_sem, c1_s, c1_r, rn_s, rn_r, own_sem, x_r, d_r, mat_s, f_s, f_r, b_s, b_r, o_s, o_r, s_s, s_r,
):
    leaf = lax.axis_index("leaf")
    sec = lax.axis_index("sec")

    def at(leaf_mask, sec_mask):
        return (leaf ^ leaf_mask, sec ^ sec_mask)

    def send(src, dst, send_sem, recv_sem, leaf_mask, sec_mask):
        pltpu.make_async_remote_copy(
            src_ref=src, dst_ref=dst, send_sem=send_sem, recv_sem=recv_sem,
            device_id=at(leaf_mask, sec_mask), device_id_type=MESH,
        ).start()

    def wait(ref, sem):
        pltpu.make_async_copy(ref, ref, sem).wait()

    barrier = pltpu.get_barrier_semaphore()
    peers = [(1, m) for m in SEC_PEERS] + [(0, m) for m in SEC_PEERS] + [(m, 0) for m in reversed(NEAR[3])]
    for leaf_mask, sec_mask in peers:
        pl.semaphore_signal(barrier, inc=1, device_id=at(leaf_mask, sec_mask), device_id_type=MESH)

    edge = ROWS - SEP
    loads = [
        (rhs, rhs_v),
        (leaf_inv.at[pl.ds(edge, SEP)], d_v.at[pl.ds(edge, SEP)]),
        (leaf_inv.at[pl.ds(0, edge)], d_v.at[pl.ds(0, edge)]),
        (noise, noise_v),
    ]
    for i, (src, dst) in enumerate(loads):
        pltpu.make_async_copy(src, dst, ld_sem.at[i]).start()

    def loaded(i):
        pltpu.make_async_copy(loads[i][0], loads[i][1], ld_sem.at[i]).wait()

    place = lax.broadcasted_iota(jnp.int32, (128, 128), 0) + 32 * (sec & 3)
    lane = lax.broadcasted_iota(jnp.int32, (128, 128), 1)
    turn = jnp.where(lane == (place & 127), F32(1), F32(0)).astype(BF)
    turn_edge = turn[:SEP]
    first = jnp.concatenate([sep_rhs[0], sep_rhs[1], sep_rhs[2], sep_noise[0]], axis=0)
    second = jnp.concatenate([sep_noise[1], sep_noise[2]], axis=0)
    rn_src[:, :128] = dot(first, turn, 0, 0).astype(BF)
    rn_src[:, 128:] = dot(second, turn[: 2 * SEP], 0, 0).astype(BF)
    mine = pl.ds(pl.multiple_of(sec * SAMP, SAMP), SAMP)
    rn_buf[sec] = rn_src[mine, :]

    dead = ROWS - blocks[0, 0] * BLOCK
    row_id = lax.broadcasted_iota(jnp.int32, (ROWS, 128), 0)
    loaded(0)
    rhs_v[...] = jnp.where(row_id >= dead, rhs_v[...].astype(F32), F32(0)).astype(BF)
    loaded(1)
    live_edge = lax.broadcasted_iota(jnp.int32, (SEP, 128), 0) + edge >= dead
    y_edge = dot(d_v[pl.ds(edge, SEP), :], rhs_v[...], 1, 0)
    y_edge = jnp.where(live_edge, y_edge, F32(0)).astype(BF)
    c1_src[...] = dot(y_edge, turn_edge, 0, 0).astype(BF)
    c1_buf[sec] = c1_src[mine, :]

    pl.semaphore_wait(barrier, len(peers))

    def part(ref, sec_mask):
        return ref.at[pl.ds(pl.multiple_of((sec ^ sec_mask) * SAMP, SAMP), SAMP)]

    for leaf_mask in (1, 0):
        for m in SEC_PEERS + ((0,) if leaf_mask else ()):
            send(part(c1_src, m), c1_buf.at[SECS * leaf_mask + sec], c1_s, c1_r, leaf_mask, m)
    for m in SEC_PEERS:
        send(part(rn_src, m), rn_buf.at[sec], rn_s, rn_r, 0, m)

    chunks = []
    for height, (p, q) in enumerate(((p1, q1), (p2, q2), (p3, q3)), 1):
        cols = pl.ds((2**height - 2) * SPAN, 2**height * SPAN)
        chunks += [(sep_panel.at[:, cols], p), (sep_inv.at[:, cols], q)]

    def rows_of(sec_mask):
        return pl.ds(pl.multiple_of((sec ^ sec_mask) * SEP, SEP), SEP)

    for j, (src, dst) in enumerate(chunks):
        for i, m in enumerate(X_PEERS):
            send(src, dst.at[rows_of(0)], mat_s.at[j], x_r.at[j, i], 0, m)
        send(src, dst.at[rows_of(0)], mat_s.at[j], d_r.at[j], 0, 1)
        pltpu.make_async_copy(src, dst.at[rows_of(0)], own_sem.at[j]).start()

    def forward(j):
        dst = chunks[j][1]
        for i, m in enumerate(X_PEERS):
            block = dst.at[rows_of(m)]
            wait(block, x_r.at[j, i])
            send(block, block, mat_s.at[j], d_r.at[j], 0, 1)

    def ready(j):
        src, dst = chunks[j]
        pltpu.make_async_copy(src, dst.at[rows_of(0)], own_sem.at[j]).wait()
        wait(dst.at[pl.ds(0, 4 * SEP)], d_r.at[j])
        return dst

    loaded(2)
    loaded(3)
    for t in range(4):
        rows = pl.ds(256 * t, 256)
        live = lax.broadcasted_iota(jnp.int32, (256, 128), 0) + 256 * t
        y = dot(d_v[rows, :], rhs_v[...], 1, 0).astype(BF).astype(F32)
        w = y + noise_v[rows, :].astype(F32)
        w_v[rows, :] = jnp.where((live >= dead) & (live < edge), w, F32(0)).astype(BF)
    for t in range(4):
        rows = pl.ds(256 * t, 256)
        x_v[rows, :] = dot(d_v[:, rows], w_v[...], 0, 0)
    eye = lax.broadcasted_iota(jnp.int32, (128, 128), 0) == lane
    for t in range(8):
        rows = pl.ds(128 * t, 128)
        diag = jnp.where(eye, jnp.broadcast_to(dev[t : t + 1, :].astype(F32), (128, 128)), F32(0))
        live = lax.broadcasted_iota(jnp.int32, (128, 128), 0) + 128 * t >= dead
        scale = jnp.broadcast_to(jnp.sum(diag, axis=1, keepdims=True), (128, 128))
        scale_v[rows, :] = jnp.where(live, scale, F32(0))

    wait(rn_buf.at[pl.ds(0, 7)], rn_r)
    group = lax.broadcasted_iota(jnp.int32, (SAMP, 128), 1) // SEP
    for item in range(6):
        tile, j = item // 4, item % 4
        for half in range(2):
            got = jnp.zeros((SAMP, 128), F32)
            for s in range(4):
                piece = rn_buf[4 * half + s, :, 128 * tile : 128 * tile + 128].astype(F32)
                got = jnp.where(group == (j + s) % 4, piece, got)
            if j:
                got = pltpu.roll(got, 128 - SEP * j, 1)
            item_v[item, :, 128 * half : 128 * half + 128] = got

    forward(0)
    wait(c1_buf.at[pl.ds(0, 15)], c1_r)

    def cols_of(height, mask):
        return pl.ds(pl.multiple_of(((leaf ^ mask) & (2**height - 1)) * SPAN, SPAN), SPAN)

    def publish(e, height, value):
        f_buf[e, 0] = value
        for m in reversed(NEAR[height]):
            send(f_buf.at[e, 0], f_buf.at[e, m], f_s.at[e], f_r.at[e, m], m, 0)

    def gathered_product(e, height, j):
        matrix = ready(j)
        total = dot(f_buf[e, 0], matrix[:, cols_of(height, 0)], 1, 1)
        for m in NEAR[height]:
            wait(f_buf.at[e, m], f_r.at[e, m])
            total += dot(f_buf[e, m], matrix[:, cols_of(height, m)], 1, 1)
        return total

    matrix = ready(0)
    total = jnp.zeros((SAMP, SPAN), F32)
    for leaf_mask in range(2):
        halves = []
        for half in range(2):
            pieces = [c1_buf[SECS * leaf_mask + 4 * half + s].astype(F32) for s in range(4)]
            halves.append((pieces[0] + pieces[1]) + (pieces[2] + pieces[3]))
        child = jnp.concatenate(halves, axis=1).astype(BF)
        total += dot(child, matrix[:, cols_of(1, leaf_mask)], 1, 1)
    solved = []
    for height in range(1, 4):
        if height > 1:
            total = gathered_product(2 * height - 3, height, 2 * height - 2)
        publish(2 * height - 2, height, (item_v[height - 1] - total).astype(BF))
        forward(2 * height - 1)
        y = gathered_product(2 * height - 2, height, 2 * height - 1).astype(BF)
        solved.append(y)
        if height < 3:
            publish(2 * height - 1, height + 1, y)
            forward(2 * height)

    def scattered_product(e, height, j, vector):
        matrix = chunks[j][1]
        for m in reversed(NEAR[height]):
            b_src[e, m] = dot(vector, matrix[:, cols_of(height, m)], 1, 0).astype(BF)
            send(b_src.at[e, m], b_buf.at[e, m], b_s.at[e], b_r.at[e, m], m, 0)
        total = dot(vector, matrix[:, cols_of(height, 0)], 1, 0)
        for m in NEAR[height]:
            wait(b_buf.at[e, m], b_r.at[e, m])
            total += b_buf[e, m].astype(F32)
        return total

    def half_of(ref, mask):
        start = pl.multiple_of(((sec ^ mask) >> 2) * 128, 128)
        return ref.at[:, pl.ds(start, 128)]

    def give_back(level, value):
        for half in range(2):
            o_src[level, half] = value[:, 128 * half : 128 * half + 128]
        o_buf[level, sec] = o_src[level, sec >> 2]
        for m in SEC_PEERS:
            send(o_src.at[level, (sec ^ m) >> 2], o_buf.at[level, sec], o_s.at[level], o_r.at[level], 0, m)

    def write_sample(level):
        wait(o_buf.at[level, pl.ds(0, 7)], o_r.at[level])
        flat = o_buf[level].reshape(128, 128)
        mine = dot(turn_edge, flat, 1, 1)
        row = jnp.broadcast_to(sep_dev[level : level + 1, :].astype(F32), (SEP, SEP))
        small = lax.broadcasted_iota(jnp.int32, (SEP, SEP), 0) == lax.broadcasted_iota(jnp.int32, (SEP, SEP), 1)
        scale = jnp.sum(jnp.where(small, row, F32(0)), axis=1, keepdims=True)
        sep_out[level] = (jnp.broadcast_to(scale, (SEP, 128)) * mine).astype(BF)

    minus = None
    e = 0
    for height in range(3, 0, -1):
        summed = solved[height - 1].astype(F32) + item_v[2 + height]
        if minus is not None:
            summed = summed - minus
        backed = scattered_product(e, height, 2 * height - 1, summed.astype(BF)).astype(BF)
        e += 1
        if height > 1:
            minus = scattered_product(e, height, 2 * height - 2, backed)
            e += 1
            give_back(height - 1, backed)
    for leaf_mask in (1, 0):
        pushed = dot(backed, p1[:, cols_of(1, leaf_mask)], 1, 0).astype(BF)
        for half in range(2):
            s_src[leaf_mask, half] = pushed[:, 128 * half : 128 * half + 128]
        for m in SEC_PEERS + ((0,) if leaf_mask else ()):
            send(s_src.at[leaf_mask, (sec ^ m) >> 2], s_buf.at[SECS * leaf_mask + sec], s_s, s_r, leaf_mask, m)
    s_buf[sec] = s_src[0, sec >> 2]
    give_back(0, backed)
    write_sample(2)
    write_sample(1)
    wait(s_buf.at[pl.ds(0, 15)], s_r)
    s0 = dot(turn_edge, s_buf[0:8].reshape(128, 128), 1, 1) + dot(turn_edge, s_buf[8:16].reshape(128, 128), 1, 1)
    w_edge = y_edge.astype(F32) + noise_v[pl.ds(edge, SEP), :].astype(F32) - s0
    w_edge = jnp.where(live_edge, w_edge, F32(0)).astype(BF)
    for t in range(4):
        rows = pl.ds(256 * t, 256)
        x = x_v[rows, :] + dot(d_v[pl.ds(edge, SEP), rows], w_edge, 0, 0)
        out[rows, :] = (scale_v[rows, :] * x).astype(BF)
    write_sample(0)

    wait(c1_buf.at[pl.ds(0, 15)], c1_s)
    wait(rn_buf.at[pl.ds(0, 7)], rn_s)
    for j, (_, dst) in enumerate(chunks):
        wait(dst.at[pl.ds(0, 7 * SEP)], mat_s.at[j])
    for e, height in enumerate((1, 2, 2, 3, 3)):
        wait(f_buf.at[e, pl.ds(0, 2**height - 1)], f_s.at[e])
    for e, height in enumerate((3, 3, 2, 2, 1)):
        wait(b_buf.at[e, pl.ds(0, 2**height - 1)], b_s.at[e])
    for level in range(3):
        wait(o_buf.at[level, pl.ds(0, 7)], o_s.at[level])
    wait(s_buf.at[pl.ds(0, 15)], s_s)


def on_device(leaf_inv, blocks, rhs, noise, dev, sep_inv, sep_panel, sep_rhs, sep_noise, sep_dev):
    dma = pltpu.SemaphoreType.DMA
    vmem = pltpu.VMEM
    anywhere = pl.BlockSpec(memory_space=pl.ANY)
    held = pl.BlockSpec(memory_space=vmem)
    scratch = [
        vmem((ROWS, ROWS), BF), vmem((ROWS, 128), BF), vmem((ROWS, 128), BF), vmem((ROWS, 128), BF),
        vmem((ROWS, 128), F32), vmem((ROWS, 128), F32),
    ]
    for height in (1, 2, 3):
        scratch += [vmem((SPAN, 2**height * SPAN), BF)] * 2
    scratch += [
        vmem((128, 128), BF), vmem((2 * SECS, SAMP, 128), BF),
        vmem((128, 256), BF), vmem((SECS, SAMP, 256), BF), vmem((6, SAMP, SPAN), F32),
        vmem((5, 8, SAMP, SPAN), BF), vmem((5, 8, SAMP, SPAN), BF), vmem((5, 8, SAMP, SPAN), BF),
        vmem((3, 2, SAMP, 128), BF), vmem((3, SECS, SAMP, 128), BF),
        vmem((2, 2, SAMP, 128), BF), vmem((2 * SECS, SAMP, 128), BF),
    ]
    scratch += [
        dma((4,)), dma, dma, dma, dma, dma((6,)), dma((6, 3)), dma((6,)), dma((6,)),
        dma((5,)), dma((5, 8)), dma((5,)), dma((5, 8)), dma((3,)), dma((3,)), dma, dma,
    ]
    return pl.pallas_call(
        kernel,
        out_shape=(
            jax.ShapeDtypeStruct(rhs.shape, BF),
            jax.ShapeDtypeStruct(sep_rhs.shape, BF),
        ),
        in_specs=[
            anywhere, pl.BlockSpec(memory_space=pltpu.SMEM), anywhere, anywhere, held,
            anywhere, anywhere, held, held, held,
        ],
        out_specs=(held, held),
        scratch_shapes=scratch,
        compiler_params=pltpu.CompilerParams(
            collective_id=0, has_side_effects=True, vmem_limit_bytes=40 * 2**20
        ),
    )(leaf_inv, blocks, rhs, noise, dev.reshape(8, 128), sep_inv, sep_panel, sep_rhs, sep_noise, sep_dev)


def solution(mesh):
    both = ("leaf", "sec")
    in_specs = (
        P(both, None), P("leaf", "sec"), P(both, None), P(both, None), P(both),
        P(both, None), P(both, None), P(None, both, None), P(None, both, None), P(None, both),
    )
    return jax.shard_map(
        on_device, mesh=mesh, in_specs=in_specs,
        out_specs=(P(both, None), P(None, both, None)), check_vma=False,
    )
```

```python
import functools

import jax
import jax.numpy as jnp
from jax import lax
from jax.experimental import pallas as pl
from jax.experimental.pallas import tpu as pltpu
from jax.sharding import PartitionSpec as P

MESH = pl.DeviceIdType.MESH
BLOCK = 128
BF = jnp.bfloat16
F32 = jnp.float32
ROWS = 1024
SEP = 32
SECS = 8
SPAN = SECS * SEP
SAMP = 16
NEAR = {1: (1,), 2: (1, 3, 2), 3: (1, 3, 4, 2, 5, 7, 6)}
SEC_PEERS = (6, 4, 7, 5, 2, 3, 1)
X_PEERS = (2, 6, 4)


def dot(a, b, ca, cb):
    return lax.dot_general(a, b, (((ca,), (cb,)), ((), ())), preferred_element_type=F32)


def kernel(
    leaf_inv, blocks_h, rhs, noise, dev_h, sep_inv, sep_panel, sep_rhs_h, sep_noise_h, sep_dev_h,
    out, sep_out,
    blocks, dev, sep_rhs, sep_noise, sep_dev, d_v, rhs_v, noise_v, w_v, x_v, scale_v,
    p1, q1, p2, q2, p3, q3,
    c1_src, c1_buf, rn_src, rn_buf, rp_buf, item_v, f_buf, b_src, b_buf, b_wide, b_near, o_src, o_buf, s_src, s_buf,
    ld_sem, c1_s, c1_r, rn_s, rn_r, rp_s, rp_r, own_sem, x_r, d_r, mat_s, f_s, f_r, b_s, b_r, w_s, w_r,
    o_s, o_r, s_s, s_r,
):
    leaf = lax.axis_index("leaf")
    sec = lax.axis_index("sec")

    def at(leaf_mask, sec_mask):
        return (leaf ^ leaf_mask, sec ^ sec_mask)

    def send(src, dst, send_sem, recv_sem, leaf_mask, sec_mask):
        pltpu.make_async_remote_copy(
            src_ref=src, dst_ref=dst, send_sem=send_sem, recv_sem=recv_sem,
            device_id=at(leaf_mask, sec_mask), device_id_type=MESH,
        ).start()

    def wait(ref, sem):
        pltpu.make_async_copy(ref, ref, sem).wait()

    barrier = pltpu.get_barrier_semaphore()
    peers = [(1, m) for m in SEC_PEERS] + [(0, m) for m in SEC_PEERS] + [(m, 0) for m in reversed(NEAR[3])]
    for leaf_mask, sec_mask in peers:
        pl.semaphore_signal(barrier, inc=1, device_id=at(leaf_mask, sec_mask), device_id_type=MESH)

    edge = ROWS - SEP
    loads = [
        (rhs, rhs_v),
        (leaf_inv.at[pl.ds(edge, SEP)], d_v.at[pl.ds(edge, SEP)]),
        (leaf_inv.at[pl.ds(0, edge)], d_v.at[pl.ds(0, edge)]),
        (noise, noise_v),
        (sep_rhs_h, sep_rhs),
        (sep_noise_h, sep_noise),
        (blocks_h, blocks),
        (dev_h, dev),
        (sep_dev_h, sep_dev),
    ]
    for i in (6, 0, 1, 4, 5, 2, 3, 7, 8):
        src, dst = loads[i]
        pltpu.make_async_copy(src, dst, ld_sem.at[i]).start()

    def loaded(i):
        pltpu.make_async_copy(loads[i][0], loads[i][1], ld_sem.at[i]).wait()

    place = lax.broadcasted_iota(jnp.int32, (128, 128), 0) + 32 * (sec & 3)
    lane = lax.broadcasted_iota(jnp.int32, (128, 128), 1)
    turn = jnp.where(lane == (place & 127), F32(1), F32(0)).astype(BF)
    turn_edge = turn[:SEP]
    mine = pl.ds(pl.multiple_of(sec * SAMP, SAMP), SAMP)

    loaded(6)
    dead = ROWS - blocks[0, 0] * BLOCK
    row_id = lax.broadcasted_iota(jnp.int32, (ROWS, 128), 0)
    loaded(0)
    rhs_v[...] = jnp.where(row_id >= dead, rhs_v[...].astype(F32), F32(0)).astype(BF)
    loaded(1)
    live_edge = lax.broadcasted_iota(jnp.int32, (SEP, 128), 0) + edge >= dead
    y_edge = dot(d_v[pl.ds(edge, SEP), :], rhs_v[...], 1, 0)
    y_edge = jnp.where(live_edge, y_edge, F32(0)).astype(BF)
    c1_src[...] = dot(y_edge, turn_edge, 0, 0).astype(BF)
    c1_buf[sec] = c1_src[mine, :]

    loaded(4)
    loaded(5)
    first = jnp.concatenate([sep_rhs[0], sep_noise[0], sep_rhs[1], sep_rhs[2]], axis=0)
    second = jnp.concatenate([sep_noise[1], sep_noise[2]], axis=0)
    rn_src[:, :128] = dot(first, turn, 0, 0).astype(BF)
    rn_src[:, 128:] = dot(second, turn[: 2 * SEP], 0, 0).astype(BF)
    rn_buf[sec] = rn_src[mine, :]

    pl.semaphore_wait(barrier, len(peers))

    def part(ref, sec_mask):
        return ref.at[pl.ds(pl.multiple_of((sec ^ sec_mask) * SAMP, SAMP), SAMP)]

    for leaf_mask in (1, 0):
        for m in SEC_PEERS + ((0,) if leaf_mask else ()):
            send(part(c1_src, m), c1_buf.at[SECS * leaf_mask + sec], c1_s, c1_r, leaf_mask, m)
    for m in SEC_PEERS + (0,):
        send(part(rn_src.at[:, pl.ds(0, 128)], m), rp_buf.at[sec], rp_s, rp_r, 1, m)
    for m in SEC_PEERS:
        send(part(rn_src, m), rn_buf.at[sec], rn_s, rn_r, 0, m)

    chunks = []
    for height, (p, q) in enumerate(((p1, q1), (p2, q2), (p3, q3)), 1):
        cols = pl.ds((2**height - 2) * SPAN, 2**height * SPAN)
        chunks += [(sep_panel.at[:, cols], p), (sep_inv.at[:, cols], q)]

    def rows_of(j, leaf_mask, sec_mask):
        start = (sec ^ sec_mask) * SEP
        if j < 2:
            start += ((leaf ^ leaf_mask) & 1) * SPAN
        return pl.ds(pl.multiple_of(start, SEP), SEP)

    def sources(j):
        return [(0, m) for m in X_PEERS] + ([(1, m) for m in (0,) + X_PEERS] if j < 2 else [])

    for j, (src, dst) in enumerate(chunks):
        own = dst.at[rows_of(j, 0, 0)]
        for i, (leaf_mask, sec_mask) in enumerate(sources(j)):
            send(src, own, mat_s.at[j], x_r.at[j, i], leaf_mask, sec_mask)
        send(src, own, mat_s.at[j], d_r.at[j], 0, 1)
        pltpu.make_async_copy(src, own, own_sem.at[j]).start()

    def forward(j):
        dst = chunks[j][1]
        for i, (leaf_mask, sec_mask) in enumerate(sources(j)):
            block = dst.at[rows_of(j, leaf_mask, sec_mask)]
            wait(block, x_r.at[j, i])
            send(block, block, mat_s.at[j], d_r.at[j], 0, 1)

    def ready(j):
        src, dst = chunks[j]
        pltpu.make_async_copy(src, dst.at[rows_of(j, 0, 0)], own_sem.at[j]).wait()
        wait(dst.at[pl.ds(0, (len(sources(j)) + 1) * SEP)], d_r.at[j])
        return dst

    loaded(2)
    loaded(3)
    loaded(7)
    loaded(8)
    for t in range(4):
        rows = pl.ds(256 * t, 256)
        live = lax.broadcasted_iota(jnp.int32, (256, 128), 0) + 256 * t
        y = dot(d_v[rows, :], rhs_v[...], 1, 0).astype(BF).astype(F32)
        w = y + noise_v[rows, :].astype(F32)
        w_v[rows, :] = jnp.where((live >= dead) & (live < edge), w, F32(0)).astype(BF)
    for t in range(4):
        rows = pl.ds(256 * t, 256)
        x_v[rows, :] = dot(d_v[:, rows], w_v[...], 0, 0)
    eye = lax.broadcasted_iota(jnp.int32, (128, 128), 0) == lane
    for t in range(8):
        rows = pl.ds(128 * t, 128)
        diag = jnp.where(eye, jnp.broadcast_to(dev[t : t + 1, :].astype(F32), (128, 128)), F32(0))
        live = lax.broadcasted_iota(jnp.int32, (128, 128), 0) + 128 * t >= dead
        scale = jnp.broadcast_to(jnp.sum(diag, axis=1, keepdims=True), (128, 128))
        scale_v[rows, :] = jnp.where(live, scale, F32(0))

    wait(rn_buf.at[pl.ds(0, 7)], rn_r)
    wait(rp_buf, rp_r)
    group = lax.broadcasted_iota(jnp.int32, (SAMP, 128), 1) // SEP

    def unpack(item, buf, tile, j):
        for half in range(2):
            got = jnp.zeros((SAMP, 128), F32)
            for s in range(4):
                piece = buf[4 * half + s, :, 128 * tile : 128 * tile + 128].astype(F32)
                got = jnp.where(group == (j + s) % 4, piece, got)
            if j:
                got = pltpu.roll(got, 128 - SEP * j, 1)
            item_v[item, :, 128 * half : 128 * half + 128] = got

    for item, (buf, tile, j) in enumerate(
        ((rn_buf, 0, 0), (rp_buf, 0, 0), (rn_buf, 0, 2), (rn_buf, 0, 3),
         (rn_buf, 0, 1), (rp_buf, 0, 1), (rn_buf, 1, 0), (rn_buf, 1, 1))
    ):
        unpack(item, buf, tile, j)

    forward(0)
    forward(1)
    wait(c1_buf.at[pl.ds(0, 15)], c1_r)

    def cols_of(height, mask):
        return pl.ds(pl.multiple_of(((leaf ^ mask) & (2**height - 1)) * SPAN, SPAN), SPAN)

    def publish(e, height, value):
        f_buf[e, 0] = value
        for m in reversed(NEAR[height]):
            send(f_buf.at[e, 0], f_buf.at[e, m], f_s.at[e], f_r.at[e, m], m, 0)

    def gathered_product(e, height, j):
        matrix = ready(j)
        total = dot(f_buf[e, 0], matrix[:, cols_of(height, 0)], 1, 1)
        for m in NEAR[height]:
            wait(f_buf.at[e, m], f_r.at[e, m])
            total += dot(f_buf[e, m], matrix[:, cols_of(height, m)], 1, 1)
        return total

    def pair_block(matrix, row_mask, col_mask):
        return matrix[cols_of(1, row_mask), cols_of(1, col_mask)]

    children = []
    for leaf_mask in range(2):
        halves = []
        for half in range(2):
            pieces = [c1_buf[SECS * leaf_mask + 4 * half + s].astype(F32) for s in range(4)]
            halves.append((pieces[0] + pieces[1]) + (pieces[2] + pieces[3]))
        children.append(jnp.concatenate(halves, axis=1).astype(BF))
    ready(0)
    reduced = []
    for m in range(2):
        total = dot(children[0], pair_block(p1, m, 0), 1, 1) + dot(children[1], pair_block(p1, m, 1), 1, 1)
        reduced.append((item_v[m] - total).astype(BF))
    ready(1)
    first_solved = []
    for m in range(2):
        total = dot(reduced[0], pair_block(q1, m, 0), 1, 1) + dot(reduced[1], pair_block(q1, m, 1), 1, 1)
        first_solved.append(total.astype(BF))
        f_buf[0, m] = first_solved[m]
    send(f_buf.at[0, pl.ds(0, 2)], f_buf.at[0, pl.ds(2, 2)], f_s.at[0], f_r.at[0, 0], 3, 0)
    forward(2)

    matrix = ready(2)
    total = dot(f_buf[0, 0], matrix[:, cols_of(2, 0)], 1, 1) + dot(f_buf[0, 1], matrix[:, cols_of(2, 1)], 1, 1)
    wait(f_buf.at[0, pl.ds(2, 2)], f_r.at[0, 0])
    total += dot(f_buf[0, 2], matrix[:, cols_of(2, 3)], 1, 1) + dot(f_buf[0, 3], matrix[:, cols_of(2, 2)], 1, 1)
    publish(1, 2, (item_v[2] - total).astype(BF))
    forward(3)
    second_solved = gathered_product(1, 2, 3).astype(BF)
    publish(2, 3, second_solved)
    forward(4)
    total = gathered_product(2, 3, 4)
    publish(3, 3, (item_v[3] - total).astype(BF))
    forward(5)
    third_solved = gathered_product(3, 3, 5).astype(BF)

    def scattered_product(e, height, j, vector):
        matrix = chunks[j][1]
        for m in reversed(NEAR[height]):
            b_src[e, m] = dot(vector, matrix[:, cols_of(height, m)], 1, 0).astype(BF)
            send(b_src.at[e, m], b_buf.at[e, m], b_s.at[e], b_r.at[e, m], m, 0)
        total = dot(vector, matrix[:, cols_of(height, 0)], 1, 0)
        for m in NEAR[height]:
            wait(b_buf.at[e, m], b_r.at[e, m])
            total += b_buf[e, m].astype(F32)
        return total

    def give_back(level, value):
        for half in range(2):
            o_src[level, half] = value[:, 128 * half : 128 * half + 128]
        o_buf[level, sec] = o_src[level, sec >> 2]
        for m in SEC_PEERS:
            send(o_src.at[level, (sec ^ m) >> 2], o_buf.at[level, sec], o_s.at[level], o_r.at[level], 0, m)

    def write_sample(level):
        wait(o_buf.at[level, pl.ds(0, 7)], o_r.at[level])
        flat = o_buf[level].reshape(128, 128)
        mine = dot(turn_edge, flat, 1, 1)
        row = jnp.broadcast_to(sep_dev[level : level + 1, :].astype(F32), (SEP, SEP))
        small = lax.broadcasted_iota(jnp.int32, (SEP, SEP), 0) == lax.broadcasted_iota(jnp.int32, (SEP, SEP), 1)
        scale = jnp.sum(jnp.where(small, row, F32(0)), axis=1, keepdims=True)
        sep_out[level] = (jnp.broadcast_to(scale, (SEP, 128)) * mine).astype(BF)

    vector = (third_solved.astype(F32) + item_v[7]).astype(BF)
    backed = scattered_product(0, 3, 5, vector).astype(BF)
    minus = scattered_product(1, 3, 4, backed)
    give_back(2, backed)
    vector = (second_solved.astype(F32) + item_v[6] - minus).astype(BF)
    backed = scattered_product(2, 2, 3, vector).astype(BF)
    blocks_out = {}
    for m in (2, 3, 1, 0):
        blocks_out[m] = dot(backed, p2[:, cols_of(2, m)], 1, 0)
        b_wide[m] = blocks_out[m].astype(BF)
    for m in (2, 3, 1):
        send(b_wide.at[m], b_near.at[m, 0], w_s, w_r.at[m], m, 0)
        send(b_wide.at[m ^ 1], b_near.at[m, 1], w_s, w_r.at[m], m, 0)
    sums = [blocks_out[0], blocks_out[1]]
    for m in (1, 3, 2):
        wait(b_near.at[m], w_r.at[m])
        for n in range(2):
            sums[n] += b_near[m, n].astype(F32)
    give_back(1, backed)
    vectors = [(first_solved[m].astype(F32) + item_v[4 + m] - sums[m]).astype(BF) for m in range(2)]
    backs = []
    for m in range(2):
        total = dot(vectors[0], pair_block(q1, 0, m), 1, 0) + dot(vectors[1], pair_block(q1, 1, m), 1, 0)
        backs.append(total.astype(BF))
    pushed = dot(backs[0], pair_block(p1, 0, 0), 1, 0) + dot(backs[1], pair_block(p1, 1, 0), 1, 0)
    for half in range(2):
        s_src[half] = pushed[:, 128 * half : 128 * half + 128].astype(BF)
    for m in SEC_PEERS:
        send(s_src.at[(sec ^ m) >> 2], s_buf.at[sec], s_s, s_r, 0, m)
    s_buf[sec] = s_src[sec >> 2]
    backed = backs[0]
    give_back(0, backed)
    write_sample(2)
    write_sample(1)
    wait(s_buf.at[pl.ds(0, 7)], s_r)
    s0 = dot(turn_edge, s_buf[...].reshape(128, 128), 1, 1)
    w_edge = y_edge.astype(F32) + noise_v[pl.ds(edge, SEP), :].astype(F32) - s0
    w_edge = jnp.where(live_edge, w_edge, F32(0)).astype(BF)
    for t in range(4):
        rows = pl.ds(256 * t, 256)
        x = x_v[rows, :] + dot(d_v[pl.ds(edge, SEP), rows], w_edge, 0, 0)
        out[rows, :] = (scale_v[rows, :] * x).astype(BF)
    write_sample(0)

    wait(c1_buf.at[pl.ds(0, 15)], c1_s)
    wait(rn_buf.at[pl.ds(0, 7)], rn_s)
    wait(rp_buf, rp_s)
    for j, (_, dst) in enumerate(chunks):
        wait(dst.at[pl.ds(0, (2 * len(sources(j)) + 1) * SEP)], mat_s.at[j])
    wait(f_buf.at[0, pl.ds(0, 2)], f_s.at[0])
    for e, height in ((1, 2), (2, 3), (3, 3)):
        wait(f_buf.at[e, pl.ds(0, 2**height - 1)], f_s.at[e])
    for e, height in ((0, 3), (1, 3), (2, 2)):
        wait(b_buf.at[e, pl.ds(0, 2**height - 1)], b_s.at[e])
    wait(b_near.at[pl.ds(0, 3)], w_s)
    for level in range(3):
        wait(o_buf.at[level, pl.ds(0, 7)], o_s.at[level])
    wait(s_buf.at[pl.ds(0, 7)], s_s)


def hand_out(leaf_made, sep_made, leaf_out, sep_out, sem):
    pairs = ((leaf_made, leaf_out), (sep_made, sep_out))
    for i, (src, dst) in enumerate(pairs):
        pltpu.make_async_copy(src, dst, sem.at[i]).start()
    for i, (src, dst) in enumerate(pairs):
        pltpu.make_async_copy(src, dst, sem.at[i]).wait()


def on_device(leaf_inv, blocks, rhs, noise, dev, sep_inv, sep_panel, sep_rhs, sep_noise, sep_dev):
    dma = pltpu.SemaphoreType.DMA
    vmem = pltpu.VMEM
    anywhere = pl.BlockSpec(memory_space=pltpu.HBM)
    held = pl.BlockSpec(memory_space=vmem)
    scratch = [
        pltpu.SMEM((1, 1), jnp.int32), vmem((8, 128), BF), vmem((3, SEP, 128), BF), vmem((3, SEP, 128), BF), vmem((3, SEP), BF),
        vmem((ROWS, ROWS), BF), vmem((ROWS, 128), BF), vmem((ROWS, 128), BF), vmem((ROWS, 128), BF),
        vmem((ROWS, 128), F32), vmem((ROWS, 128), F32),
    ]
    for height in (1, 2, 3):
        scratch += [vmem((SPAN * (2 if height == 1 else 1), 2**height * SPAN), BF)] * 2
    scratch += [
        vmem((128, 128), BF), vmem((2 * SECS, SAMP, 128), BF),
        vmem((128, 256), BF), vmem((SECS, SAMP, 256), BF), vmem((SECS, SAMP, 128), BF), vmem((8, SAMP, SPAN), F32),
        vmem((4, 8, SAMP, SPAN), BF), vmem((3, 8, SAMP, SPAN), BF), vmem((3, 8, SAMP, SPAN), BF),
        vmem((4, SAMP, SPAN), BF), vmem((4, 2, SAMP, SPAN), BF),
        vmem((3, 2, SAMP, 128), BF), vmem((3, SECS, SAMP, 128), BF),
        vmem((2, SAMP, 128), BF), vmem((SECS, SAMP, 128), BF),
    ]
    scratch += [
        dma((9,)), dma, dma, dma, dma, dma, dma, dma((6,)), dma((6, 7)), dma((6,)), dma((6,)),
        dma((4,)), dma((4, 8)), dma((3,)), dma((3, 8)), dma, dma((4,)), dma((3,)), dma((3,)), dma, dma,
    ]
    operands = [leaf_inv, rhs, noise, dev.reshape(8, 128), sep_inv, sep_panel, sep_rhs, sep_noise, sep_dev]
    operands = [pltpu.with_memory_space_constraint(a, pltpu.HBM) for a in operands]
    results = (jax.ShapeDtypeStruct(rhs.shape, BF), jax.ShapeDtypeStruct(sep_rhs.shape, BF))
    made = pl.pallas_call(
        kernel,
        out_shape=results,
        in_specs=[anywhere] * 10,
        out_specs=(held, held),
        scratch_shapes=scratch,
        compiler_params=pltpu.CompilerParams(
            collective_id=0, has_side_effects=True, vmem_limit_bytes=30 * 2**20
        ),
    )(operands[0], blocks, *operands[1:])
    return pl.pallas_call(
        hand_out,
        out_shape=results,
        in_specs=[pl.BlockSpec(memory_space=pl.ANY)] * 2,
        out_specs=[pl.BlockSpec(memory_space=pl.ANY)] * 2,
        scratch_shapes=[dma((2,))],
        compiler_params=pltpu.CompilerParams(vmem_limit_bytes=2**20),
    )(*made)


def solution(mesh):
    both = ("leaf", "sec")
    in_specs = (
        P(both, None), P("leaf", "sec"), P(both, None), P(both, None), P(both),
        P(both, None), P(both, None), P(None, both, None), P(None, both, None), P(None, both),
    )
    return jax.shard_map(
        on_device, mesh=mesh, in_specs=in_specs,
        out_specs=(P(both, None), P(None, both, None)), check_vma=False,
    )
```

```python
import functools

import jax
import jax.numpy as jnp
from jax import lax
from jax.experimental import pallas as pl
from jax.experimental.pallas import tpu as pltpu
from jax.sharding import PartitionSpec as P

MESH = pl.DeviceIdType.MESH
BLOCK = 128
BF = jnp.bfloat16
F32 = jnp.float32
ROWS = 1024
SEP = 32
SECS = 8
SPAN = SECS * SEP
SAMP = 16
NEAR = {1: (1,), 2: (1, 3, 2), 3: (1, 3, 4, 2, 5, 7, 6)}
SEC_PEERS = (6, 4, 7, 5, 2, 3, 1)
PAIR = ((1, 0), (0, 2), (0, 6), (0, 4), (1, 2), (1, 6), (1, 4))
GREET = ((1, 4), (1, 2), (1, 6), (0, 4), (1, 0), (0, 2), (0, 6), (3, 0), (4, 0), (0, 1))


def dot(a, b, ca, cb):
    return lax.dot_general(a, b, (((ca,), (cb,)), ((), ())), preferred_element_type=F32)


def kernel(
    leaf_inv, blocks_h, rhs, noise, dev_h, sep_inv, sep_panel, sep_rhs_h, sep_noise_h, sep_dev_h,
    out, sep_out,
    blocks, dev, sep_rhs, sep_noise, sep_dev, d_v, rhs_v, noise_v, w_v, x_v, scale_v,
    p1, q1, p2, q2, p3, q3,
    e_src, e_got, e_mix, own_buf, pair_buf, item_v, f_buf, b_src, b_buf, b_wide, b_near, o_src, o_buf, s_src, s_buf,
    ld_sem, swap_s, swap_r, line_s, line_r, pair_s, pair_r, own_sem, x_r, d_r, mat_s, f_s, f_r, b_s, b_r, w_s, w_r,
    o_s, o_r, s_s, s_r,
):
    leaf = lax.axis_index("leaf")
    sec = lax.axis_index("sec")

    def at(leaf_mask, sec_mask):
        return (leaf ^ leaf_mask, sec ^ sec_mask)

    def send(src, dst, send_sem, recv_sem, leaf_mask, sec_mask):
        pltpu.make_async_remote_copy(
            src_ref=src, dst_ref=dst, send_sem=send_sem, recv_sem=recv_sem,
            device_id=at(leaf_mask, sec_mask), device_id_type=MESH,
        ).start()

    def wait(ref, sem):
        pltpu.make_async_copy(ref, ref, sem).wait()

    barrier = pltpu.get_barrier_semaphore()
    for leaf_mask, sec_mask in GREET:
        pl.semaphore_signal(barrier, inc=1, device_id=at(leaf_mask, sec_mask), device_id_type=MESH)

    edge = ROWS - SEP
    loads = [
        (rhs, rhs_v),
        (leaf_inv.at[pl.ds(edge, SEP)], d_v.at[pl.ds(edge, SEP)]),
        (leaf_inv.at[pl.ds(0, edge)], d_v.at[pl.ds(0, edge)]),
        (noise, noise_v),
        (sep_rhs_h, sep_rhs),
        (sep_noise_h, sep_noise),
        (blocks_h, blocks),
        (dev_h, dev),
        (sep_dev_h, sep_dev),
    ]
    for i in (6, 0, 1, 4, 5, 2, 3, 7, 8):
        src, dst = loads[i]
        pltpu.make_async_copy(src, dst, ld_sem.at[i]).start()

    def loaded(i):
        pltpu.make_async_copy(loads[i][0], loads[i][1], ld_sem.at[i]).wait()

    core, chip = sec & 1, sec >> 1
    k = lax.broadcasted_iota(jnp.int32, (2 * SEP, 128), 0)
    place = (k & 31) + SEP * core + 64 * (((k >> 5) + chip) & 1)
    lane = lax.broadcasted_iota(jnp.int32, (2 * SEP, 128), 1)
    turn = jnp.where(lane == place, F32(1), F32(0)).astype(BF)
    turn_edge = turn[:SEP]

    loaded(6)
    dead = ROWS - blocks[0, 0] * BLOCK
    row_id = lax.broadcasted_iota(jnp.int32, (ROWS, 128), 0)
    loaded(0)
    rhs_v[...] = jnp.where(row_id >= dead, rhs_v[...].astype(F32), F32(0)).astype(BF)
    loaded(1)
    live_edge = lax.broadcasted_iota(jnp.int32, (SEP, 128), 0) + edge >= dead
    y_edge = dot(d_v[pl.ds(edge, SEP), :], rhs_v[...], 1, 0)
    y_edge = jnp.where(live_edge, y_edge, F32(0)).astype(BF)
    loaded(4)
    loaded(5)
    e_src[:, :, :, :128] = dot(y_edge, turn_edge, 0, 0).astype(BF).reshape(4, 2, SAMP, 128)
    for tile, rows in enumerate(((sep_rhs[0], sep_noise[0]), (sep_rhs[1], sep_rhs[2]), (sep_noise[1], sep_noise[2])), 1):
        turned = dot(jnp.concatenate(rows, axis=0), turn, 0, 0).astype(BF)
        e_src[:, :, :, 128 * tile : 128 * tile + 128] = turned.reshape(4, 2, SAMP, 128)

    pl.semaphore_wait(barrier, len(GREET))
    send(e_src.at[:, 1 - core], e_got, swap_s, swap_r, 0, 1)

    chunks = []
    for height, (p, q) in enumerate(((p1, q1), (p2, q2), (p3, q3)), 1):
        cols = pl.ds((2**height - 2) * SPAN, 2**height * SPAN)
        chunks += [(sep_panel.at[:, cols], p), (sep_inv.at[:, cols], q)]

    chunks.append(chunks[1])

    def sources(j):
        return PAIR if j == 0 else (PAIR[:1] + PAIR[4:] if j == 6 else PAIR[1:4])

    def rows_of(j, leaf_mask, sec_mask):
        start = (sec ^ sec_mask) * SEP
        if j in (0, 1, 6):
            start += ((leaf ^ leaf_mask) & 1) * SPAN
        return pl.ds(pl.multiple_of(start, SEP), SEP)

    def spread(j):
        src, dst = chunks[j]
        own = dst.at[rows_of(j, 0, 0)]
        for i, (leaf_mask, sec_mask) in enumerate(sources(j)):
            send(src, own, mat_s.at[j], x_r.at[j, i], leaf_mask, sec_mask)
        if j < 6:
            send(src, own, mat_s.at[j], d_r.at[j], 0, 1)
            pltpu.make_async_copy(src, own, own_sem.at[j]).start()

    def forward(j):
        for i, (leaf_mask, sec_mask) in enumerate(sources(j)):
            block = chunks[j][1].at[rows_of(j, leaf_mask, sec_mask)]
            wait(block, x_r.at[j, i])
            send(block, block, mat_s.at[j], d_r.at[j], 0, 1)

    def ready(j):
        src, dst = chunks[j]
        if j < 6:
            pltpu.make_async_copy(src, dst.at[rows_of(j, 0, 0)], own_sem.at[j]).wait()
        wait(dst.at[pl.ds(0, (len(sources(j)) + (j < 6)) * SEP)], d_r.at[j])
        return dst

    spread(0)
    spread(1)

    def give_edge(leaf_mask, sec_mask):
        src = e_mix.at[chip ^ (sec_mask >> 1)]
        if leaf_mask:
            send(src.at[:, pl.ds(0, 256)], pair_buf.at[chip], pair_s, pair_r, leaf_mask, sec_mask)
        else:
            send(src, own_buf.at[chip], line_s, line_r, leaf_mask, sec_mask)

    wait(e_got, swap_r)
    e_mix[...] = (e_src[:, core].astype(F32) + e_got[...].astype(F32)).astype(BF)
    own_buf[chip] = e_mix[chip]
    for leaf_mask, sec_mask in reversed(PAIR):
        give_edge(leaf_mask, sec_mask)
    for j in range(2, 7):
        spread(j)
    forward(0)
    forward(1)

    def leaf_solve():
        loaded(2)
        loaded(3)
        for t in range(4):
            rows = pl.ds(256 * t, 256)
            live = lax.broadcasted_iota(jnp.int32, (256, 128), 0) + 256 * t
            y = dot(d_v[rows, :], rhs_v[...], 1, 0).astype(BF).astype(F32)
            w = y + noise_v[rows, :].astype(F32)
            w_v[rows, :] = jnp.where((live >= dead) & (live < edge), w, F32(0)).astype(BF)

    def leaf_back():
        for t in range(4):
            rows = pl.ds(256 * t, 256)
            x_v[rows, :] = dot(d_v[:, rows], w_v[...], 0, 0)

    def leaf_scale():
        loaded(7)
        loaded(8)
        row = lax.broadcasted_iota(jnp.int32, (128, 128), 0)
        eye = row == lax.broadcasted_iota(jnp.int32, (128, 128), 1)
        for t in range(8):
            diag = jnp.where(eye, jnp.broadcast_to(dev[t : t + 1, :].astype(F32), (128, 128)), F32(0))
            scale = jnp.broadcast_to(jnp.sum(diag, axis=1, keepdims=True), (128, 128))
            scale_v[pl.ds(128 * t, 128), :] = jnp.where(row + 128 * t >= dead, scale, F32(0))

    wait(own_buf.at[pl.ds(0, 3)], line_r)
    wait(pair_buf, pair_r)
    group = lax.broadcasted_iota(jnp.int32, (SAMP, 128), 1) // 64

    def unpack(item, buf, tile, f):
        cols = slice(128 * tile, 128 * tile + 128)
        for half in range(2):
            got = jnp.where(group == f, buf[2 * half, :, cols].astype(F32), buf[2 * half + 1, :, cols].astype(F32))
            if f:
                got = pltpu.roll(got, 64, 1)
            item_v[item, :, 128 * half : 128 * half + 128] = got

    children = []
    for buf in (own_buf, pair_buf):
        tiles = [buf[c, :, :128].astype(F32) for c in range(4)]
        children.append(jnp.concatenate([tiles[0] + tiles[1], tiles[2] + tiles[3]], axis=1).astype(BF))
    for item, (buf, tile, f) in enumerate(
        ((own_buf, 1, 0), (pair_buf, 1, 0), (own_buf, 2, 0), (own_buf, 2, 1),
         (own_buf, 1, 1), (pair_buf, 1, 1), (own_buf, 3, 0), (own_buf, 3, 1))
    ):
        unpack(item, buf, tile, f)

    def cols_of(height, mask):
        return pl.ds(pl.multiple_of(((leaf ^ mask) & (2**height - 1)) * SPAN, SPAN), SPAN)

    def publish(e, height, value):
        f_buf[e, 0] = value
        for m in reversed(NEAR[height]):
            send(f_buf.at[e, 0], f_buf.at[e, m], f_s.at[e], f_r.at[e, m], m, 0)

    def gathered_product(e, height, j):
        matrix = ready(j)
        total = dot(f_buf[e, 0], matrix[:, cols_of(height, 0)], 1, 1)
        for part in (NEAR[height][:3], NEAR[height][3:]):
            for m in part:
                wait(f_buf.at[e, m], f_r.at[e, m])
            for m in part:
                total += dot(f_buf[e, m], matrix[:, cols_of(height, m)], 1, 1)
        return total

    def pair_block(matrix, row_mask, col_mask):
        return matrix[cols_of(1, row_mask), cols_of(1, col_mask)]

    ready(0)
    reduced = []
    for m in range(2):
        total = dot(children[0], pair_block(p1, m, 0), 1, 1) + dot(children[1], pair_block(p1, m, 1), 1, 1)
        reduced.append((item_v[m] - total).astype(BF))
    ready(1)
    total = dot(reduced[0], pair_block(q1, 0, 0), 1, 1) + dot(reduced[1], pair_block(q1, 0, 1), 1, 1)
    first_solved = total.astype(BF)
    publish(0, 2, first_solved)
    forward(2)

    total = gathered_product(0, 2, 2)
    publish(1, 2, (item_v[2] - total).astype(BF))
    forward(3)

    leaf_solve()
    second_solved = gathered_product(1, 2, 3).astype(BF)
    publish(2, 3, second_solved)
    forward(4)

    leaf_back()
    total = gathered_product(2, 3, 4)
    publish(3, 3, (item_v[3] - total).astype(BF))
    forward(5)

    forward(6)
    leaf_scale()
    third_solved = gathered_product(3, 3, 5).astype(BF)

    def scattered_product(e, height, j, vector):
        matrix = chunks[j][1]
        for part in (NEAR[height][3:], NEAR[height][:3]):
            for m in reversed(part):
                b_src[e, m] = dot(vector, matrix[:, cols_of(height, m)], 1, 0).astype(BF)
            for m in reversed(part):
                send(b_src.at[e, m], b_buf.at[e, m], b_s.at[e], b_r.at[e, m], m, 0)
        total = dot(vector, matrix[:, cols_of(height, 0)], 1, 0)
        for m in NEAR[height]:
            wait(b_buf.at[e, m], b_r.at[e, m])
            total += b_buf[e, m].astype(F32)
        return total

    def give_back(level, value):
        i = level - 1
        for half in range(2):
            o_src[i, half] = value[:, 128 * half : 128 * half + 128]
        o_buf[i, sec] = o_src[i, sec >> 2]
        for m in SEC_PEERS:
            send(o_src.at[i, (sec ^ m) >> 2], o_buf.at[i, sec], o_s.at[i], o_r.at[i], 0, m)

    def put_sample(level, flat):
        mine = dot(turn_edge, flat, 1, 1)
        row = jnp.broadcast_to(sep_dev[level : level + 1, :].astype(F32), (SEP, SEP))
        small = lax.broadcasted_iota(jnp.int32, (SEP, SEP), 0) == lax.broadcasted_iota(jnp.int32, (SEP, SEP), 1)
        scale = jnp.sum(jnp.where(small, row, F32(0)), axis=1, keepdims=True)
        sep_out[level] = (jnp.broadcast_to(scale, (SEP, 128)) * mine).astype(BF)

    def write_sample(level):
        wait(o_buf.at[level - 1, pl.ds(0, 7)], o_r.at[level - 1])
        put_sample(level, o_buf[level - 1].reshape(128, 128))

    vector = (third_solved.astype(F32) + item_v[7]).astype(BF)
    backed = scattered_product(0, 3, 5, vector).astype(BF)
    minus = scattered_product(1, 3, 4, backed)
    give_back(2, backed)
    vector = (second_solved.astype(F32) + item_v[6] - minus).astype(BF)
    backed = scattered_product(2, 2, 3, vector).astype(BF)
    blocks_out = {}
    for m in (2, 3, 1, 0):
        blocks_out[m] = dot(backed, p2[:, cols_of(2, m)], 1, 0)
        b_wide[m] = blocks_out[m].astype(BF)
    for m in (2, 3, 1):
        send(b_wide.at[m], b_near.at[m, 0], w_s, w_r.at[m], m, 0)
        send(b_wide.at[m ^ 1], b_near.at[m, 1], w_s, w_r.at[m], m, 0)
    sums = [blocks_out[0], blocks_out[1]]
    for m in (1, 3, 2):
        wait(b_near.at[m], w_r.at[m])
        for n in range(2):
            sums[n] += b_near[m, n].astype(F32)
    give_back(1, backed)
    ready(6)
    vectors = [(f_buf[0, m].astype(F32) + item_v[4 + m] - sums[m]).astype(BF) for m in range(2)]
    backs = []
    for m in range(2):
        total = dot(vectors[0], pair_block(q1, 0, m), 1, 0) + dot(vectors[1], pair_block(q1, 1, m), 1, 0)
        backs.append(total.astype(BF))
    pushed = dot(backs[0], pair_block(p1, 0, 0), 1, 0) + dot(backs[1], pair_block(p1, 1, 0), 1, 0)
    for half in range(2):
        s_src[half, 0] = pushed[:, 128 * half : 128 * half + 128].astype(BF)
        s_src[half, 1] = backs[0][:, 128 * half : 128 * half + 128]
    for m in SEC_PEERS:
        send(s_src.at[(sec ^ m) >> 2], s_buf.at[sec], s_s, s_r, 0, m)
    s_buf[sec] = s_src[sec >> 2]
    write_sample(2)
    write_sample(1)
    wait(e_got, swap_s)
    wait(own_buf.at[pl.ds(0, 3)], line_s)
    wait(pair_buf, pair_s)
    for j, (_, dst) in enumerate(chunks):
        wait(dst.at[pl.ds(0, (2 * len(sources(j)) + (j < 6)) * SEP)], mat_s.at[j])
    for e, height in ((0, 2), (1, 2), (2, 3), (3, 3)):
        wait(f_buf.at[e, pl.ds(0, 2**height - 1)], f_s.at[e])
    for e, height in ((0, 3), (1, 3), (2, 2)):
        wait(b_buf.at[e, pl.ds(0, 2**height - 1)], b_s.at[e])
    wait(b_near.at[pl.ds(0, 3)], w_s)
    for level in (1, 2):
        wait(o_buf.at[level - 1, pl.ds(0, 7)], o_s.at[level - 1])
    wait(s_buf.at[pl.ds(0, 7)], s_r)
    s0 = dot(turn_edge, s_buf[:, 0].reshape(128, 128), 1, 1)
    w_edge = y_edge.astype(F32) + noise_v[pl.ds(edge, SEP), :].astype(F32) - s0
    w_edge = jnp.where(live_edge, w_edge, F32(0)).astype(BF)
    for t in range(4):
        rows = pl.ds(256 * t, 256)
        x = x_v[rows, :] + dot(d_v[pl.ds(edge, SEP), rows], w_edge, 0, 0)
        out[rows, :] = (scale_v[rows, :] * x).astype(BF)
    put_sample(0, s_buf[:, 1].reshape(128, 128))
    wait(s_buf.at[pl.ds(0, 7)], s_s)


def hand_out(leaf_made, sep_made, leaf_out, sep_out, sem):
    pairs = ((leaf_made, leaf_out), (sep_made, sep_out))
    for i, (src, dst) in enumerate(pairs):
        pltpu.make_async_copy(src, dst, sem.at[i]).start()
    for i, (src, dst) in enumerate(pairs):
        pltpu.make_async_copy(src, dst, sem.at[i]).wait()


def on_device(leaf_inv, blocks, rhs, noise, dev, sep_inv, sep_panel, sep_rhs, sep_noise, sep_dev):
    dma = pltpu.SemaphoreType.DMA
    vmem = pltpu.VMEM
    anywhere = pl.BlockSpec(memory_space=pltpu.HBM)
    held = pl.BlockSpec(memory_space=vmem)
    scratch = [
        pltpu.SMEM((1, 1), jnp.int32), vmem((8, 128), BF), vmem((3, SEP, 128), BF), vmem((3, SEP, 128), BF), vmem((3, SEP), BF),
        vmem((ROWS, ROWS), BF), vmem((ROWS, 128), BF), vmem((ROWS, 128), BF), vmem((ROWS, 128), BF),
        vmem((ROWS, 128), F32), vmem((ROWS, 128), F32),
    ]
    for height in (1, 2, 3):
        scratch += [vmem((SPAN * (2 if height == 1 else 1), 2**height * SPAN), BF)] * 2
    scratch += [
        vmem((4, 2, SAMP, 512), BF), vmem((4, SAMP, 512), BF), vmem((4, SAMP, 512), BF), vmem((4, SAMP, 512), BF),
        vmem((4, SAMP, 256), BF), vmem((8, SAMP, SPAN), F32),
        vmem((4, 8, SAMP, SPAN), BF), vmem((3, 8, SAMP, SPAN), BF), vmem((3, 8, SAMP, SPAN), BF),
        vmem((4, SAMP, SPAN), BF), vmem((4, 2, SAMP, SPAN), BF),
        vmem((2, 2, SAMP, 128), BF), vmem((2, SECS, SAMP, 128), BF),
        vmem((2, 2, SAMP, 128), BF), vmem((SECS, 2, SAMP, 128), BF),
    ]
    scratch += [
        dma((9,)), dma, dma, dma, dma, dma, dma, dma((6,)), dma((7, 7)), dma((7,)), dma((7,)),
        dma((4,)), dma((4, 8)), dma((3,)), dma((3, 8)), dma, dma((4,)), dma((2,)), dma((2,)), dma, dma,
    ]
    operands = [leaf_inv, rhs, noise, dev.reshape(8, 128), sep_inv, sep_panel, sep_rhs, sep_noise, sep_dev]
    operands = [pltpu.with_memory_space_constraint(a, pltpu.HBM) for a in operands]
    results = (jax.ShapeDtypeStruct(rhs.shape, BF), jax.ShapeDtypeStruct(sep_rhs.shape, BF))
    made = pl.pallas_call(
        kernel,
        out_shape=results,
        in_specs=[anywhere] * 10,
        out_specs=(held, held),
        scratch_shapes=scratch,
        compiler_params=pltpu.CompilerParams(
            collective_id=0, has_side_effects=True, vmem_limit_bytes=30 * 2**20
        ),
    )(operands[0], blocks, *operands[1:])
    return pl.pallas_call(
        hand_out,
        out_shape=results,
        in_specs=[pl.BlockSpec(memory_space=pl.ANY)] * 2,
        out_specs=[pl.BlockSpec(memory_space=pl.ANY)] * 2,
        scratch_shapes=[dma((2,))],
        compiler_params=pltpu.CompilerParams(vmem_limit_bytes=2**20),
    )(*made)


def solution(mesh):
    both = ("leaf", "sec")
    in_specs = (
        P(both, None), P("leaf", "sec"), P(both, None), P(both, None), P(both),
        P(both, None), P(both, None), P(None, both, None), P(None, both, None), P(None, both),
    )
    return jax.shard_map(
        on_device, mesh=mesh, in_specs=in_specs,
        out_specs=(P(both, None), P(None, both, None)), check_vma=False,
    )
```

```python
import functools

import jax
import jax.numpy as jnp
from jax import lax
from jax.experimental import pallas as pl
from jax.experimental.pallas import tpu as pltpu
from jax.sharding import PartitionSpec as P

MESH = pl.DeviceIdType.MESH
BLOCK = 128
BF = jnp.bfloat16
F32 = jnp.float32
ROWS = 1024
SEP = 32
SECS = 8
SPAN = SECS * SEP
SAMP = 16
NEAR = {1: (1,), 2: (1, 3, 2), 3: (1, 3, 4, 2, 5, 7, 6)}
SEC_PEERS = (6, 4, 7, 5, 2, 3, 1)
PAIR = ((1, 0), (0, 2), (0, 6), (0, 4), (1, 2), (1, 6), (1, 4))
GREET = ((1, 4), (1, 2), (1, 6), (0, 4), (1, 0), (0, 2), (0, 6), (3, 0), (4, 0), (0, 1))


def dot(a, b, ca, cb):
    return lax.dot_general(a, b, (((ca,), (cb,)), ((), ())), preferred_element_type=F32)


def kernel(
    leaf_inv, blocks_h, rhs, noise, dev_h, sep_inv, sep_panel, sep_rhs_h, sep_noise_h, sep_dev_h,
    out, sep_out,
    blocks, dev, sep_rhs, sep_noise, sep_dev, d_v, rhs_v, noise_v, w_v, x_v, scale_v,
    p1, q1, p2, q2, p3, q3,
    e_src, e_got, e_mix, own_buf, pair_buf, item_v, f_buf, b_src, b_buf, b_wide, b_near, o_src, o_buf, s_src, s_buf,
    ld_sem, swap_s, swap_r, line_s, line_r, pair_s, pair_r, own_sem, x_r, d_r, mat_s, f_s, f_r, b_s, b_r, w_s, w_r,
    o_s, o_r, s_s, s_r,
):
    leaf = lax.axis_index("leaf")
    sec = lax.axis_index("sec")

    def at(leaf_mask, sec_mask):
        return (leaf ^ leaf_mask, sec ^ sec_mask)

    def send(src, dst, send_sem, recv_sem, leaf_mask, sec_mask):
        pltpu.make_async_remote_copy(
            src_ref=src, dst_ref=dst, send_sem=send_sem, recv_sem=recv_sem,
            device_id=at(leaf_mask, sec_mask), device_id_type=MESH,
        ).start()

    def wait(ref, sem):
        pltpu.make_async_copy(ref, ref, sem).wait()

    barrier = pltpu.get_barrier_semaphore()
    for leaf_mask, sec_mask in GREET:
        pl.semaphore_signal(barrier, inc=1, device_id=at(leaf_mask, sec_mask), device_id_type=MESH)

    edge = ROWS - SEP
    loads = [
        (rhs, rhs_v),
        (leaf_inv.at[pl.ds(edge, SEP)], d_v.at[pl.ds(edge, SEP)]),
        (leaf_inv.at[pl.ds(0, edge)], d_v.at[pl.ds(0, edge)]),
        (noise, noise_v),
        (sep_rhs_h, sep_rhs),
        (sep_noise_h, sep_noise),
        (blocks_h, blocks),
        (dev_h, dev),
        (sep_dev_h, sep_dev),
    ]
    for i in (6, 0, 1, 4, 5, 2, 3, 7, 8):
        src, dst = loads[i]
        pltpu.make_async_copy(src, dst, ld_sem.at[i]).start()

    def loaded(i):
        pltpu.make_async_copy(loads[i][0], loads[i][1], ld_sem.at[i]).wait()

    core, chip = sec & 1, sec >> 1
    k = lax.broadcasted_iota(jnp.int32, (2 * SEP, 128), 0)
    place = (k & 31) + SEP * core + 64 * (((k >> 5) + chip) & 1)
    lane = lax.broadcasted_iota(jnp.int32, (2 * SEP, 128), 1)
    turn = jnp.where(lane == place, F32(1), F32(0)).astype(BF)
    turn_edge = turn[:SEP]

    loaded(6)
    dead = ROWS - blocks[0, 0] * BLOCK
    row_id = lax.broadcasted_iota(jnp.int32, (ROWS, 128), 0)
    loaded(0)
    rhs_v[...] = jnp.where(row_id >= dead, rhs_v[...].astype(F32), F32(0)).astype(BF)
    loaded(1)
    live_edge = lax.broadcasted_iota(jnp.int32, (SEP, 128), 0) + edge >= dead
    y_edge = dot(d_v[pl.ds(edge, SEP), :], rhs_v[...], 1, 0)
    y_edge = jnp.where(live_edge, y_edge, F32(0)).astype(BF)
    loaded(4)
    loaded(5)
    e_src[:, :, :, :128] = dot(y_edge, turn_edge, 0, 0).astype(BF).reshape(4, 2, SAMP, 128)
    for tile, rows in enumerate(((sep_rhs[0], sep_noise[0]), (sep_rhs[1], sep_rhs[2]), (sep_noise[1], sep_noise[2])), 1):
        turned = dot(jnp.concatenate(rows, axis=0), turn, 0, 0).astype(BF)
        e_src[:, :, :, 128 * tile : 128 * tile + 128] = turned.reshape(4, 2, SAMP, 128)

    pl.semaphore_wait(barrier, len(GREET))
    send(e_src.at[:, 1 - core], e_got, swap_s, swap_r, 0, 1)

    chunks = []
    for height, (p, q) in enumerate(((p1, q1), (p2, q2), (p3, q3)), 1):
        cols = pl.ds((2**height - 2) * SPAN, 2**height * SPAN)
        chunks += [(sep_panel.at[:, cols], p), (sep_inv.at[:, cols], q)]

    chunks.append(chunks[1])

    def sources(j):
        return PAIR if j == 0 else (PAIR[:1] + PAIR[4:] if j == 6 else PAIR[1:4])

    def rows_of(j, leaf_mask, sec_mask):
        start = (sec ^ sec_mask) * SEP
        if j in (0, 1, 6):
            start += ((leaf ^ leaf_mask) & 1) * SPAN
        return pl.ds(pl.multiple_of(start, SEP), SEP)

    def spread(j):
        src, dst = chunks[j]
        own = dst.at[rows_of(j, 0, 0)]
        for i, (leaf_mask, sec_mask) in enumerate(sources(j)):
            send(src, own, mat_s.at[j], x_r.at[j, i], leaf_mask, sec_mask)
        if j < 6:
            send(src, own, mat_s.at[j], d_r.at[j], 0, 1)
            pltpu.make_async_copy(src, own, own_sem.at[j]).start()

    def forward(j):
        for i, (leaf_mask, sec_mask) in enumerate(sources(j)):
            block = chunks[j][1].at[rows_of(j, leaf_mask, sec_mask)]
            wait(block, x_r.at[j, i])
            send(block, block, mat_s.at[j], d_r.at[j], 0, 1)

    def ready(j):
        src, dst = chunks[j]
        if j < 6:
            pltpu.make_async_copy(src, dst.at[rows_of(j, 0, 0)], own_sem.at[j]).wait()
        wait(dst.at[pl.ds(0, (len(sources(j)) + (j < 6)) * SEP)], d_r.at[j])
        return dst

    spread(0)
    spread(1)

    def give_edge(leaf_mask, sec_mask):
        src = e_mix.at[chip ^ (sec_mask >> 1)]
        if leaf_mask:
            send(src.at[:, pl.ds(0, 256)], pair_buf.at[chip], pair_s, pair_r, leaf_mask, sec_mask)
        else:
            send(src, own_buf.at[chip], line_s, line_r, leaf_mask, sec_mask)

    wait(e_got, swap_r)
    e_mix[...] = (e_src[:, core].astype(F32) + e_got[...].astype(F32)).astype(BF)
    own_buf[chip] = e_mix[chip]
    for leaf_mask, sec_mask in reversed(PAIR):
        give_edge(leaf_mask, sec_mask)
    for j in range(2, 7):
        spread(j)
    forward(0)
    forward(1)

    def leaf_solve():
        loaded(2)
        loaded(3)
        for t in range(4):
            rows = pl.ds(256 * t, 256)
            live = lax.broadcasted_iota(jnp.int32, (256, 128), 0) + 256 * t
            y = dot(d_v[rows, :], rhs_v[...], 1, 0).astype(BF).astype(F32)
            w = y + noise_v[rows, :].astype(F32)
            w_v[rows, :] = jnp.where((live >= dead) & (live < edge), w, F32(0)).astype(BF)

    def leaf_back():
        for t in range(4):
            rows = pl.ds(256 * t, 256)
            x_v[rows, :] = dot(d_v[:, rows], w_v[...], 0, 0)

    def leaf_scale():
        loaded(7)
        loaded(8)
        row = lax.broadcasted_iota(jnp.int32, (128, 128), 0)
        eye = row == lax.broadcasted_iota(jnp.int32, (128, 128), 1)
        for t in range(8):
            diag = jnp.where(eye, jnp.broadcast_to(dev[t : t + 1, :].astype(F32), (128, 128)), F32(0))
            scale = jnp.broadcast_to(jnp.sum(diag, axis=1, keepdims=True), (128, 128))
            scale_v[pl.ds(128 * t, 128), :] = jnp.where(row + 128 * t >= dead, scale, F32(0))

    wait(own_buf.at[pl.ds(0, 3)], line_r)
    wait(pair_buf, pair_r)
    group = lax.broadcasted_iota(jnp.int32, (SAMP, 128), 1) // 64

    def unpack(item, buf, tile, f):
        cols = slice(128 * tile, 128 * tile + 128)
        for half in range(2):
            got = jnp.where(group == f, buf[2 * half, :, cols].astype(F32), buf[2 * half + 1, :, cols].astype(F32))
            if f:
                got = pltpu.roll(got, 64, 1)
            item_v[item, :, 128 * half : 128 * half + 128] = got

    children = []
    for buf in (own_buf, pair_buf):
        tiles = [buf[c, :, :128].astype(F32) for c in range(4)]
        children.append(jnp.concatenate([tiles[0] + tiles[1], tiles[2] + tiles[3]], axis=1).astype(BF))
    unpack(0, own_buf, 1, 0)
    unpack(1, pair_buf, 1, 0)

    def cols_of(height, mask):
        return pl.ds(pl.multiple_of(((leaf ^ mask) & (2**height - 1)) * SPAN, SPAN), SPAN)

    def publish(e, height, value):
        f_buf[e, 0] = value
        for m in reversed(NEAR[height]):
            send(f_buf.at[e, 0], f_buf.at[e, m], f_s.at[e], f_r.at[e, m], m, 0)

    def gathered_product(e, height, j):
        matrix = ready(j)
        total = dot(f_buf[e, 0], matrix[:, cols_of(height, 0)], 1, 1)
        for part in (NEAR[height][:3], NEAR[height][3:]):
            for m in part:
                wait(f_buf.at[e, m], f_r.at[e, m])
            for m in part:
                total += dot(f_buf[e, m], matrix[:, cols_of(height, m)], 1, 1)
        return total

    def pair_block(matrix, row_mask, col_mask):
        return matrix[cols_of(1, row_mask), cols_of(1, col_mask)]

    ready(0)
    reduced = []
    for m in range(2):
        total = dot(children[0], pair_block(p1, m, 0), 1, 1) + dot(children[1], pair_block(p1, m, 1), 1, 1)
        reduced.append((item_v[m] - total).astype(BF))
    ready(1)
    total = dot(reduced[0], pair_block(q1, 0, 0), 1, 1) + dot(reduced[1], pair_block(q1, 0, 1), 1, 1)
    first_solved = total.astype(BF)
    publish(0, 2, first_solved)
    unpack(2, own_buf, 2, 0)
    unpack(3, own_buf, 2, 1)
    forward(2)

    total = gathered_product(0, 2, 2)
    publish(1, 2, (item_v[2] - total).astype(BF))
    forward(3)
    unpack(4, own_buf, 1, 1)
    unpack(5, pair_buf, 1, 1)
    unpack(6, own_buf, 3, 0)
    unpack(7, own_buf, 3, 1)

    leaf_solve()
    second_solved = gathered_product(1, 2, 3).astype(BF)
    publish(2, 3, second_solved)
    forward(4)

    leaf_back()
    total = gathered_product(2, 3, 4)
    publish(3, 3, (item_v[3] - total).astype(BF))
    forward(5)

    forward(6)
    leaf_scale()
    third_solved = gathered_product(3, 3, 5).astype(BF)

    def scattered_product(e, height, j, vector, meanwhile=None):
        matrix = chunks[j][1]
        for part in (NEAR[height][3:], NEAR[height][:3]):
            for m in reversed(part):
                b_src[e, m] = dot(vector, matrix[:, cols_of(height, m)], 1, 0).astype(BF)
            for m in reversed(part):
                send(b_src.at[e, m], b_buf.at[e, m], b_s.at[e], b_r.at[e, m], m, 0)
        total = dot(vector, matrix[:, cols_of(height, 0)], 1, 0)
        if meanwhile is not None:
            meanwhile()
        for m in NEAR[height]:
            wait(b_buf.at[e, m], b_r.at[e, m])
            total += b_buf[e, m].astype(F32)
        return total

    def give_back(level, value):
        i = level - 1
        for half in range(2):
            o_src[i, half] = value[:, 128 * half : 128 * half + 128]
        o_buf[i, sec] = o_src[i, sec >> 2]
        for m in SEC_PEERS:
            send(o_src.at[i, (sec ^ m) >> 2], o_buf.at[i, sec], o_s.at[i], o_r.at[i], 0, m)

    def put_sample(level, flat):
        mine = dot(turn_edge, flat, 1, 1)
        row = jnp.broadcast_to(sep_dev[level : level + 1, :].astype(F32), (SEP, SEP))
        small = lax.broadcasted_iota(jnp.int32, (SEP, SEP), 0) == lax.broadcasted_iota(jnp.int32, (SEP, SEP), 1)
        scale = jnp.sum(jnp.where(small, row, F32(0)), axis=1, keepdims=True)
        sep_out[level] = (jnp.broadcast_to(scale, (SEP, 128)) * mine).astype(BF)

    def write_sample(level):
        wait(o_buf.at[level - 1, pl.ds(0, 7)], o_r.at[level - 1])
        put_sample(level, o_buf[level - 1].reshape(128, 128))

    vector = (third_solved.astype(F32) + item_v[7]).astype(BF)
    backed = scattered_product(0, 3, 5, vector).astype(BF)
    minus = scattered_product(1, 3, 4, backed)
    vector = (second_solved.astype(F32) + item_v[6] - minus).astype(BF)
    top_backed = backed
    backed = scattered_product(2, 2, 3, vector, lambda: give_back(2, top_backed)).astype(BF)
    blocks_out = {}
    for m in (2, 3, 1, 0):
        blocks_out[m] = dot(backed, p2[:, cols_of(2, m)], 1, 0)
        b_wide[m] = blocks_out[m].astype(BF)
    for m in (2, 3, 1):
        send(b_wide.at[m], b_near.at[m, 0], w_s, w_r.at[m], m, 0)
        send(b_wide.at[m ^ 1], b_near.at[m, 1], w_s, w_r.at[m], m, 0)
    give_back(1, backed)
    sums = [blocks_out[0], blocks_out[1]]
    for m in (1, 3, 2):
        wait(b_near.at[m], w_r.at[m])
        for n in range(2):
            sums[n] += b_near[m, n].astype(F32)
    ready(6)
    vectors = [(f_buf[0, m].astype(F32) + item_v[4 + m] - sums[m]).astype(BF) for m in range(2)]
    backs = []
    for m in range(2):
        total = dot(vectors[0], pair_block(q1, 0, m), 1, 0) + dot(vectors[1], pair_block(q1, 1, m), 1, 0)
        backs.append(total.astype(BF))
    pushed = dot(backs[0], pair_block(p1, 0, 0), 1, 0) + dot(backs[1], pair_block(p1, 1, 0), 1, 0)
    for half in range(2):
        s_src[half, 0] = pushed[:, 128 * half : 128 * half + 128].astype(BF)
        s_src[half, 1] = backs[0][:, 128 * half : 128 * half + 128]
    for m in SEC_PEERS:
        send(s_src.at[(sec ^ m) >> 2], s_buf.at[sec], s_s, s_r, 0, m)
    s_buf[sec] = s_src[sec >> 2]
    write_sample(2)
    write_sample(1)
    wait(e_got, swap_s)
    wait(own_buf.at[pl.ds(0, 3)], line_s)
    wait(pair_buf, pair_s)
    for j, (_, dst) in enumerate(chunks):
        wait(dst.at[pl.ds(0, (2 * len(sources(j)) + (j < 6)) * SEP)], mat_s.at[j])
    for e, height in ((0, 2), (1, 2), (2, 3), (3, 3)):
        wait(f_buf.at[e, pl.ds(0, 2**height - 1)], f_s.at[e])
    for e, height in ((0, 3), (1, 3), (2, 2)):
        wait(b_buf.at[e, pl.ds(0, 2**height - 1)], b_s.at[e])
    wait(b_near.at[pl.ds(0, 3)], w_s)
    for level in (1, 2):
        wait(o_buf.at[level - 1, pl.ds(0, 7)], o_s.at[level - 1])
    wait(s_buf.at[pl.ds(0, 7)], s_r)
    s0 = dot(turn_edge, s_buf[:, 0].reshape(128, 128), 1, 1)
    w_edge = y_edge.astype(F32) + noise_v[pl.ds(edge, SEP), :].astype(F32) - s0
    w_edge = jnp.where(live_edge, w_edge, F32(0)).astype(BF)
    for t in range(4):
        rows = pl.ds(256 * t, 256)
        x = x_v[rows, :] + dot(d_v[pl.ds(edge, SEP), rows], w_edge, 0, 0)
        out[rows, :] = (scale_v[rows, :] * x).astype(BF)
    put_sample(0, s_buf[:, 1].reshape(128, 128))
    wait(s_buf.at[pl.ds(0, 7)], s_s)


def hand_out(leaf_made, sep_made, leaf_out, sep_out, sem):
    pairs = ((leaf_made, leaf_out), (sep_made, sep_out))
    for i, (src, dst) in enumerate(pairs):
        pltpu.make_async_copy(src, dst, sem.at[i]).start()
    for i, (src, dst) in enumerate(pairs):
        pltpu.make_async_copy(src, dst, sem.at[i]).wait()


def on_device(leaf_inv, blocks, rhs, noise, dev, sep_inv, sep_panel, sep_rhs, sep_noise, sep_dev):
    dma = pltpu.SemaphoreType.DMA
    vmem = pltpu.VMEM
    anywhere = pl.BlockSpec(memory_space=pltpu.HBM)
    held = pl.BlockSpec(memory_space=vmem)
    scratch = [
        pltpu.SMEM((1, 1), jnp.int32), vmem((8, 128), BF), vmem((3, SEP, 128), BF), vmem((3, SEP, 128), BF), vmem((3, SEP), BF),
        vmem((ROWS, ROWS), BF), vmem((ROWS, 128), BF), vmem((ROWS, 128), BF), vmem((ROWS, 128), BF),
        vmem((ROWS, 128), F32), vmem((ROWS, 128), F32),
    ]
    for height in (1, 2, 3):
        scratch += [vmem((SPAN * (2 if height == 1 else 1), 2**height * SPAN), BF)] * 2
    scratch += [
        vmem((4, 2, SAMP, 512), BF), vmem((4, SAMP, 512), BF), vmem((4, SAMP, 512), BF), vmem((4, SAMP, 512), BF),
        vmem((4, SAMP, 256), BF), vmem((8, SAMP, SPAN), F32),
        vmem((4, 8, SAMP, SPAN), BF), vmem((3, 8, SAMP, SPAN), BF), vmem((3, 8, SAMP, SPAN), BF),
        vmem((4, SAMP, SPAN), BF), vmem((4, 2, SAMP, SPAN), BF),
        vmem((2, 2, SAMP, 128), BF), vmem((2, SECS, SAMP, 128), BF),
        vmem((2, 2, SAMP, 128), BF), vmem((SECS, 2, SAMP, 128), BF),
    ]
    scratch += [
        dma((9,)), dma, dma, dma, dma, dma, dma, dma((6,)), dma((7, 7)), dma((7,)), dma((7,)),
        dma((4,)), dma((4, 8)), dma((3,)), dma((3, 8)), dma, dma((4,)), dma((2,)), dma((2,)), dma, dma,
    ]
    operands = [leaf_inv, rhs, noise, dev.reshape(8, 128), sep_inv, sep_panel, sep_rhs, sep_noise, sep_dev]
    operands = [pltpu.with_memory_space_constraint(a, pltpu.HBM) for a in operands]
    results = (jax.ShapeDtypeStruct(rhs.shape, BF), jax.ShapeDtypeStruct(sep_rhs.shape, BF))
    made = pl.pallas_call(
        kernel,
        out_shape=results,
        in_specs=[anywhere] * 10,
        out_specs=(held, held),
        scratch_shapes=scratch,
        compiler_params=pltpu.CompilerParams(
            collective_id=0, has_side_effects=True, vmem_limit_bytes=30 * 2**20
        ),
    )(operands[0], blocks, *operands[1:])
    return pl.pallas_call(
        hand_out,
        out_shape=results,
        in_specs=[pl.BlockSpec(memory_space=pl.ANY)] * 2,
        out_specs=[pl.BlockSpec(memory_space=pl.ANY)] * 2,
        scratch_shapes=[dma((2,))],
        compiler_params=pltpu.CompilerParams(vmem_limit_bytes=2**20),
    )(*made)


def solution(mesh):
    both = ("leaf", "sec")
    in_specs = (
        P(both, None), P("leaf", "sec"), P(both, None), P(both, None), P(both),
        P(both, None), P(both, None), P(None, both, None), P(None, both, None), P(None, both),
    )
    return jax.shard_map(
        on_device, mesh=mesh, in_specs=in_specs,
        out_specs=(P(both, None), P(None, both, None)), check_vma=False,
    )
```

```python
import functools

import jax
import jax.numpy as jnp
from jax import lax
from jax.experimental import pallas as pl
from jax.experimental.pallas import tpu as pltpu
from jax.sharding import PartitionSpec as P

MESH = pl.DeviceIdType.MESH
BLOCK = 128
BF = jnp.bfloat16
F32 = jnp.float32
ROWS = 1024
SEP = 32
SECS = 8
SPAN = SECS * SEP
SAMP = 16
NEAR = {1: (1,), 2: (1, 3, 2), 3: (1, 3, 4, 2, 5, 7, 6)}
SEC_PEERS = (6, 4, 7, 5, 2, 3, 1)
PAIR = ((1, 0), (0, 2), (0, 6), (0, 4), (1, 2), (1, 6), (1, 4))
GREET = ((1, 4), (1, 2), (1, 6), (0, 4), (1, 0), (0, 2), (0, 6), (3, 0), (4, 0), (0, 1))


def dot(a, b, ca, cb):
    return lax.dot_general(a, b, (((ca,), (cb,)), ((), ())), preferred_element_type=F32)


def kernel(
    leaf_inv, blocks_h, rhs, noise, dev_h, sep_inv, sep_panel, sep_rhs_h, sep_noise_h, sep_dev_h,
    out, sep_out,
    blocks, dev, sep_rhs, sep_noise, sep_dev, d_v, rhs_v, noise_v, w_v, x_v, scale_v,
    p1, q1, p2, q2, p3, q3,
    e_src, e_got, e_mix, own_buf, pair_buf, item_v, f_buf, b_src, b_buf, b_wide, b_near, o_src, o_buf, s_src, s_buf,
    ld_sem, swap_s, swap_r, line_s, line_r, pair_s, pair_r, own_sem, x_r, d_r, mat_s, f_s, f_r, b_s, b_r, w_s, w_r,
    o_s, o_r, s_s, s_r,
):
    leaf = lax.axis_index("leaf")
    sec = lax.axis_index("sec")

    def at(leaf_mask, sec_mask):
        return (leaf ^ leaf_mask, sec ^ sec_mask)

    def send(src, dst, send_sem, recv_sem, leaf_mask, sec_mask):
        pltpu.make_async_remote_copy(
            src_ref=src, dst_ref=dst, send_sem=send_sem, recv_sem=recv_sem,
            device_id=at(leaf_mask, sec_mask), device_id_type=MESH,
        ).start()

    def wait(ref, sem):
        pltpu.make_async_copy(ref, ref, sem).wait()

    barrier = pltpu.get_barrier_semaphore()
    for leaf_mask, sec_mask in GREET:
        pl.semaphore_signal(barrier, inc=1, device_id=at(leaf_mask, sec_mask), device_id_type=MESH)

    edge = ROWS - SEP
    loads = [
        (rhs, rhs_v),
        (leaf_inv.at[pl.ds(edge, SEP)], d_v.at[pl.ds(edge, SEP)]),
        (leaf_inv.at[pl.ds(0, edge)], d_v.at[pl.ds(0, edge)]),
        (noise, noise_v),
        (sep_rhs_h, sep_rhs),
        (sep_noise_h, sep_noise),
        (blocks_h, blocks),
        (dev_h, dev),
        (sep_dev_h, sep_dev),
    ]
    for i in (6, 0, 1, 4, 5, 2, 3, 7, 8):
        src, dst = loads[i]
        pltpu.make_async_copy(src, dst, ld_sem.at[i]).start()

    def loaded(i):
        pltpu.make_async_copy(loads[i][0], loads[i][1], ld_sem.at[i]).wait()

    core, chip = sec & 1, sec >> 1
    k = lax.broadcasted_iota(jnp.int32, (2 * SEP, 128), 0)
    place = (k & 31) + SEP * core + 64 * (((k >> 5) + chip) & 1)
    lane = lax.broadcasted_iota(jnp.int32, (2 * SEP, 128), 1)
    turn = jnp.where(lane == place, F32(1), F32(0)).astype(BF)
    turn_edge = turn[:SEP]

    loaded(6)
    dead = ROWS - blocks[0, 0] * BLOCK
    row_id = lax.broadcasted_iota(jnp.int32, (ROWS, 128), 0)
    loaded(0)
    rhs_v[...] = jnp.where(row_id >= dead, rhs_v[...].astype(F32), F32(0)).astype(BF)
    loaded(1)
    live_edge = lax.broadcasted_iota(jnp.int32, (SEP, 128), 0) + edge >= dead
    y_edge = dot(d_v[pl.ds(edge, SEP), :], rhs_v[...], 1, 0)
    y_edge = jnp.where(live_edge, y_edge, F32(0)).astype(BF)
    loaded(4)
    loaded(5)
    e_src[:, :, :, :128] = dot(y_edge, turn_edge, 0, 0).astype(BF).reshape(4, 2, SAMP, 128)
    for tile, rows in enumerate(((sep_rhs[0], sep_noise[0]), (sep_rhs[1], sep_rhs[2]), (sep_noise[1], sep_noise[2])), 1):
        turned = dot(jnp.concatenate(rows, axis=0), turn, 0, 0).astype(BF)
        e_src[:, :, :, 128 * tile : 128 * tile + 128] = turned.reshape(4, 2, SAMP, 128)

    pl.semaphore_wait(barrier, len(GREET))
    send(e_src.at[:, 1 - core], e_got, swap_s, swap_r, 0, 1)

    chunks = []
    for height, (p, q) in enumerate(((p1, q1), (p2, q2), (p3, q3)), 1):
        cols = pl.ds((2**height - 2) * SPAN, 2**height * SPAN)
        chunks += [(sep_panel.at[:, cols], p), (sep_inv.at[:, cols], q)]

    chunks.append(chunks[1])

    def sources(j):
        return PAIR if j == 0 else (PAIR[:1] + PAIR[4:] if j == 6 else PAIR[1:4])

    def rows_of(j, leaf_mask, sec_mask):
        start = (sec ^ sec_mask) * SEP
        if j in (0, 1, 6):
            start += ((leaf ^ leaf_mask) & 1) * SPAN
        return pl.ds(pl.multiple_of(start, SEP), SEP)

    def spread(j):
        src, dst = chunks[j]
        own = dst.at[rows_of(j, 0, 0)]
        for i, (leaf_mask, sec_mask) in enumerate(sources(j)):
            send(src, own, mat_s.at[j], x_r.at[j, i], leaf_mask, sec_mask)
        if j < 6:
            send(src, own, mat_s.at[j], d_r.at[j], 0, 1)
            pltpu.make_async_copy(src, own, own_sem.at[j]).start()

    def forward(j):
        for i, (leaf_mask, sec_mask) in enumerate(sources(j)):
            block = chunks[j][1].at[rows_of(j, leaf_mask, sec_mask)]
            wait(block, x_r.at[j, i])
            send(block, block, mat_s.at[j], d_r.at[j], 0, 1)

    def ready(j):
        src, dst = chunks[j]
        if j < 6:
            pltpu.make_async_copy(src, dst.at[rows_of(j, 0, 0)], own_sem.at[j]).wait()
        wait(dst.at[pl.ds(0, (len(sources(j)) + (j < 6)) * SEP)], d_r.at[j])
        return dst

    spread(0)
    spread(1)

    def give_edge(leaf_mask, sec_mask):
        src = e_mix.at[chip ^ (sec_mask >> 1)]
        if leaf_mask:
            send(src.at[:, pl.ds(0, 256)], pair_buf.at[chip], pair_s, pair_r, leaf_mask, sec_mask)
        else:
            send(src, own_buf.at[chip], line_s, line_r, leaf_mask, sec_mask)

    wait(e_got, swap_r)
    e_mix[...] = (e_src[:, core].astype(F32) + e_got[...].astype(F32)).astype(BF)
    own_buf[chip] = e_mix[chip]
    for leaf_mask, sec_mask in reversed(PAIR):
        give_edge(leaf_mask, sec_mask)
    for j in range(2, 7):
        spread(j)

    def leaf_solve():
        loaded(2)
        loaded(3)
        for t in range(4):
            rows = pl.ds(256 * t, 256)
            live = lax.broadcasted_iota(jnp.int32, (256, 128), 0) + 256 * t
            y = dot(d_v[rows, :], rhs_v[...], 1, 0).astype(BF).astype(F32)
            w = y + noise_v[rows, :].astype(F32)
            w_v[rows, :] = jnp.where((live >= dead) & (live < edge), w, F32(0)).astype(BF)

    def leaf_back():
        for t in range(4):
            rows = pl.ds(256 * t, 256)
            x_v[rows, :] = dot(d_v[:, rows], w_v[...], 0, 0)

    def leaf_scale():
        loaded(7)
        loaded(8)
        row = lax.broadcasted_iota(jnp.int32, (128, 128), 0)
        eye = row == lax.broadcasted_iota(jnp.int32, (128, 128), 1)
        for t in range(8):
            diag = jnp.where(eye, jnp.broadcast_to(dev[t : t + 1, :].astype(F32), (128, 128)), F32(0))
            scale = jnp.broadcast_to(jnp.sum(diag, axis=1, keepdims=True), (128, 128))
            scale_v[pl.ds(128 * t, 128), :] = jnp.where(row + 128 * t >= dead, scale, F32(0))

    wait(own_buf.at[pl.ds(0, 3)], line_r)
    wait(pair_buf, pair_r)
    group = lax.broadcasted_iota(jnp.int32, (SAMP, 128), 1) // 64

    def unpack(item, buf, tile, f):
        cols = slice(128 * tile, 128 * tile + 128)
        for half in range(2):
            got = jnp.where(group == f, buf[2 * half, :, cols].astype(F32), buf[2 * half + 1, :, cols].astype(F32))
            if f:
                got = pltpu.roll(got, 64, 1)
            item_v[item, :, 128 * half : 128 * half + 128] = got

    children = []
    for buf in (own_buf, pair_buf):
        tiles = [buf[c, :, :128].astype(F32) for c in range(4)]
        children.append(jnp.concatenate([tiles[0] + tiles[1], tiles[2] + tiles[3]], axis=1).astype(BF))
    unpack(0, own_buf, 1, 0)
    unpack(1, pair_buf, 1, 0)
    forward(0)
    forward(1)

    def cols_of(height, mask):
        return pl.ds(pl.multiple_of(((leaf ^ mask) & (2**height - 1)) * SPAN, SPAN), SPAN)

    def publish(e, height, value):
        f_buf[e, 0] = value
        for m in reversed(NEAR[height]):
            send(f_buf.at[e, 0], f_buf.at[e, m], f_s.at[e], f_r.at[e, m], m, 0)

    def gathered_product(e, height, j):
        matrix = ready(j)
        total = dot(f_buf[e, 0], matrix[:, cols_of(height, 0)], 1, 1)
        for part in (NEAR[height][:3], NEAR[height][3:]):
            for m in part:
                wait(f_buf.at[e, m], f_r.at[e, m])
            for m in part:
                total += dot(f_buf[e, m], matrix[:, cols_of(height, m)], 1, 1)
        return total

    def pair_block(matrix, row_mask, col_mask):
        return matrix[cols_of(1, row_mask), cols_of(1, col_mask)]

    ready(0)
    reduced = []
    for m in range(2):
        total = dot(children[0], pair_block(p1, m, 0), 1, 1) + dot(children[1], pair_block(p1, m, 1), 1, 1)
        reduced.append((item_v[m] - total).astype(BF))
    ready(1)
    total = dot(reduced[0], pair_block(q1, 0, 0), 1, 1) + dot(reduced[1], pair_block(q1, 0, 1), 1, 1)
    first_solved = total.astype(BF)
    publish(0, 2, first_solved)
    unpack(2, own_buf, 2, 0)
    unpack(3, own_buf, 2, 1)
    forward(2)

    total = gathered_product(0, 2, 2)
    publish(1, 2, (item_v[2] - total).astype(BF))
    forward(3)
    unpack(4, own_buf, 1, 1)
    unpack(5, pair_buf, 1, 1)
    unpack(6, own_buf, 3, 0)
    unpack(7, own_buf, 3, 1)

    leaf_solve()
    second_solved = gathered_product(1, 2, 3).astype(BF)
    publish(2, 3, second_solved)
    forward(4)

    leaf_back()
    total = gathered_product(2, 3, 4)
    publish(3, 3, (item_v[3] - total).astype(BF))
    forward(5)

    forward(6)
    leaf_scale()
    third_solved = gathered_product(3, 3, 5).astype(BF)

    def scattered_product(e, height, j, vector, meanwhile=None):
        matrix = chunks[j][1]
        for part in (NEAR[height][3:], NEAR[height][:3]):
            for m in reversed(part):
                b_src[e, m] = dot(vector, matrix[:, cols_of(height, m)], 1, 0).astype(BF)
            for m in reversed(part):
                send(b_src.at[e, m], b_buf.at[e, m], b_s.at[e], b_r.at[e, m], m, 0)
        total = dot(vector, matrix[:, cols_of(height, 0)], 1, 0)
        if meanwhile is not None:
            meanwhile()
        for m in NEAR[height]:
            wait(b_buf.at[e, m], b_r.at[e, m])
            total += b_buf[e, m].astype(F32)
        return total

    def give_back(level, value):
        i = level - 1
        for half in range(2):
            o_src[i, half] = value[:, 128 * half : 128 * half + 128]
        o_buf[i, sec] = o_src[i, sec >> 2]
        for m in SEC_PEERS:
            send(o_src.at[i, (sec ^ m) >> 2], o_buf.at[i, sec], o_s.at[i], o_r.at[i], 0, m)

    def put_sample(level, flat):
        mine = dot(turn_edge, flat, 1, 1)
        row = jnp.broadcast_to(sep_dev[level : level + 1, :].astype(F32), (SEP, SEP))
        small = lax.broadcasted_iota(jnp.int32, (SEP, SEP), 0) == lax.broadcasted_iota(jnp.int32, (SEP, SEP), 1)
        scale = jnp.sum(jnp.where(small, row, F32(0)), axis=1, keepdims=True)
        sep_out[level] = (jnp.broadcast_to(scale, (SEP, 128)) * mine).astype(BF)

    def write_sample(level):
        wait(o_buf.at[level - 1, pl.ds(0, 7)], o_r.at[level - 1])
        put_sample(level, o_buf[level - 1].reshape(128, 128))

    vector = (third_solved.astype(F32) + item_v[7]).astype(BF)
    backed = scattered_product(0, 3, 5, vector).astype(BF)
    minus = scattered_product(1, 3, 4, backed)
    vector = (second_solved.astype(F32) + item_v[6] - minus).astype(BF)
    top_backed = backed
    backed = scattered_product(2, 2, 3, vector, lambda: give_back(2, top_backed)).astype(BF)
    blocks_out = {}
    for m in (2, 3, 1, 0):
        blocks_out[m] = dot(backed, p2[:, cols_of(2, m)], 1, 0)
        b_wide[m] = blocks_out[m].astype(BF)
    for m in (2, 3, 1):
        send(b_wide.at[m], b_near.at[m, 0], w_s, w_r.at[m], m, 0)
        send(b_wide.at[m ^ 1], b_near.at[m, 1], w_s, w_r.at[m], m, 0)
    give_back(1, backed)
    sums = [blocks_out[0], blocks_out[1]]
    for m in (1, 3, 2):
        wait(b_near.at[m], w_r.at[m])
        for n in range(2):
            sums[n] += b_near[m, n].astype(F32)
    ready(6)
    vectors = [(f_buf[0, m].astype(F32) + item_v[4 + m] - sums[m]).astype(BF) for m in range(2)]
    backs = []
    for m in range(2):
        total = dot(vectors[0], pair_block(q1, 0, m), 1, 0) + dot(vectors[1], pair_block(q1, 1, m), 1, 0)
        backs.append(total.astype(BF))
    pushed = dot(backs[0], pair_block(p1, 0, 0), 1, 0) + dot(backs[1], pair_block(p1, 1, 0), 1, 0)
    for half in range(2):
        s_src[half, 0] = pushed[:, 128 * half : 128 * half + 128].astype(BF)
        s_src[half, 1] = backs[0][:, 128 * half : 128 * half + 128]
    for m in SEC_PEERS:
        send(s_src.at[(sec ^ m) >> 2], s_buf.at[sec], s_s, s_r, 0, m)
    s_buf[sec] = s_src[sec >> 2]
    write_sample(2)
    write_sample(1)
    wait(e_got, swap_s)
    wait(own_buf.at[pl.ds(0, 3)], line_s)
    wait(pair_buf, pair_s)
    for j, (_, dst) in enumerate(chunks):
        wait(dst.at[pl.ds(0, (2 * len(sources(j)) + (j < 6)) * SEP)], mat_s.at[j])
    for e, height in ((0, 2), (1, 2), (2, 3), (3, 3)):
        wait(f_buf.at[e, pl.ds(0, 2**height - 1)], f_s.at[e])
    for e, height in ((0, 3), (1, 3), (2, 2)):
        wait(b_buf.at[e, pl.ds(0, 2**height - 1)], b_s.at[e])
    wait(b_near.at[pl.ds(0, 3)], w_s)
    for level in (1, 2):
        wait(o_buf.at[level - 1, pl.ds(0, 7)], o_s.at[level - 1])
    wait(s_buf.at[pl.ds(0, 7)], s_r)
    s0 = dot(turn_edge, s_buf[:, 0].reshape(128, 128), 1, 1)
    w_edge = y_edge.astype(F32) + noise_v[pl.ds(edge, SEP), :].astype(F32) - s0
    w_edge = jnp.where(live_edge, w_edge, F32(0)).astype(BF)
    for t in range(4):
        rows = pl.ds(256 * t, 256)
        x = x_v[rows, :] + dot(d_v[pl.ds(edge, SEP), rows], w_edge, 0, 0)
        out[rows, :] = (scale_v[rows, :] * x).astype(BF)
    put_sample(0, s_buf[:, 1].reshape(128, 128))
    wait(s_buf.at[pl.ds(0, 7)], s_s)


def hand_out(leaf_made, sep_made, leaf_out, sep_out, sem):
    pairs = ((leaf_made, leaf_out), (sep_made, sep_out))
    for i, (src, dst) in enumerate(pairs):
        pltpu.make_async_copy(src, dst, sem.at[i]).start()
    for i, (src, dst) in enumerate(pairs):
        pltpu.make_async_copy(src, dst, sem.at[i]).wait()


def on_device(leaf_inv, blocks, rhs, noise, dev, sep_inv, sep_panel, sep_rhs, sep_noise, sep_dev):
    dma = pltpu.SemaphoreType.DMA
    vmem = pltpu.VMEM
    anywhere = pl.BlockSpec(memory_space=pltpu.HBM)
    held = pl.BlockSpec(memory_space=vmem)
    scratch = [
        pltpu.SMEM((1, 1), jnp.int32), vmem((8, 128), BF), vmem((3, SEP, 128), BF), vmem((3, SEP, 128), BF), vmem((3, SEP), BF),
        vmem((ROWS, ROWS), BF), vmem((ROWS, 128), BF), vmem((ROWS, 128), BF), vmem((ROWS, 128), BF),
        vmem((ROWS, 128), F32), vmem((ROWS, 128), F32),
    ]
    for height in (1, 2, 3):
        scratch += [vmem((SPAN * (2 if height == 1 else 1), 2**height * SPAN), BF)] * 2
    scratch += [
        vmem((4, 2, SAMP, 512), BF), vmem((4, SAMP, 512), BF), vmem((4, SAMP, 512), BF), vmem((4, SAMP, 512), BF),
        vmem((4, SAMP, 256), BF), vmem((8, SAMP, SPAN), F32),
        vmem((4, 8, SAMP, SPAN), BF), vmem((3, 8, SAMP, SPAN), BF), vmem((3, 8, SAMP, SPAN), BF),
        vmem((4, SAMP, SPAN), BF), vmem((4, 2, SAMP, SPAN), BF),
        vmem((2, 2, SAMP, 128), BF), vmem((2, SECS, SAMP, 128), BF),
        vmem((2, 2, SAMP, 128), BF), vmem((SECS, 2, SAMP, 128), BF),
    ]
    scratch += [
        dma((9,)), dma, dma, dma, dma, dma, dma, dma((6,)), dma((7, 7)), dma((7,)), dma((7,)),
        dma((4,)), dma((4, 8)), dma((3,)), dma((3, 8)), dma, dma((4,)), dma((2,)), dma((2,)), dma, dma,
    ]
    operands = [leaf_inv, rhs, noise, dev.reshape(8, 128), sep_inv, sep_panel, sep_rhs, sep_noise, sep_dev]
    operands = [pltpu.with_memory_space_constraint(a, pltpu.HBM) for a in operands]
    results = (jax.ShapeDtypeStruct(rhs.shape, BF), jax.ShapeDtypeStruct(sep_rhs.shape, BF))
    made = pl.pallas_call(
        kernel,
        out_shape=results,
        in_specs=[anywhere] * 10,
        out_specs=(held, held),
        scratch_shapes=scratch,
        compiler_params=pltpu.CompilerParams(
            collective_id=0, has_side_effects=True, vmem_limit_bytes=30 * 2**20
        ),
    )(operands[0], blocks, *operands[1:])
    return pl.pallas_call(
        hand_out,
        out_shape=results,
        in_specs=[pl.BlockSpec(memory_space=pl.ANY)] * 2,
        out_specs=[pl.BlockSpec(memory_space=pl.ANY)] * 2,
        scratch_shapes=[dma((2,))],
        compiler_params=pltpu.CompilerParams(vmem_limit_bytes=2**20),
    )(*made)


def solution(mesh):
    both = ("leaf", "sec")
    in_specs = (
        P(both, None), P("leaf", "sec"), P(both, None), P(both, None), P(both),
        P(both, None), P(both, None), P(None, both, None), P(None, both, None), P(None, both),
    )
    return jax.shard_map(
        on_device, mesh=mesh, in_specs=in_specs,
        out_specs=(P(both, None), P(None, both, None)), check_vma=False,
    )
```
